32 devices in a mesh: row: 8 (over y, x, core), col: 4 (over z).
Axes of the slice: x: 2, y: 2, z: 4, core: 2. Of those that a mesh axis runs over, the one named last changes fastest.
Arguments:
- rhs_rows: float32 [16384, 256], P(('row', 'col')), may hold values from -6 to 6
- dest_row: int32 [16384], P(('row', 'col')), may hold values from 0 to 16383, as said below
- diag_inverse: bfloat16 [4, 32, 128, 128], P(None, ('row', 'col')), may hold values from -1 to 1.5, as said below
- lower_blocks: bfloat16 [3, 8, 4, 128, 4, 8, 128], P(None, 'row', None, None, 'col'), may hold values from -0.09375 to 0.09375
- block_mask: int32 [3, 8, 4, 4, 8], P(None, 'row', None, 'col'), may hold values 0 or 1
Outputs:
- solution: bfloat16 [4, 32, 128, 256], P(None, ('row', 'col'))
The draws below stay inside these ranges and needn't reach their ends.
Inputs may be any that keep to these rules, and one draw needn't show every extreme that they name: dest_row is a permutation of the rows. In each aligned block of 512 entries, exactly 16 entries g have (g // 128) % 32 equal to q, for every supernode index q. `diag_inverse`: every block is lower triangular with positive diagonal entries.
All inputs are finite; a program needn't handle non-finite values. No bound on the sum of `block_mask` on one device may be relied on, other than what follows from the above.
Results may differ from the reference program's by a relative error of at most 0.029.
Values may be sent and summed in bfloat16 or wider, within the bound.
No kernel may reach another device: no remote copies, remote signals or barrier semaphores. Data moves between devices by JAX's collectives and lax.ppermute only.
A program may use at most 128 MiB of HBM per device.

```python
import math
import jax
import jax.numpy as jnp
from jax import lax

B = 128
NRHS = 256
NLEV = 4
OWNERS = 8
HOLDERS = 4
S = 32
LEVM = 3
NROWS = 16384
GROUP = 16


def draw_dest_row(key, part):
    rows_dev = NLEV * B
    key_owner, key_source = jax.random.split(key)
    owner_keys = jax.random.split(key_owner, S)
    local_perm = jax.vmap(lambda sub_key: jax.random.permutation(sub_key, rows_dev))(owner_keys)
    by_source = local_perm.reshape(S, S, GROUP).transpose(1, 0, 2)
    level_idx = by_source // B
    within = by_source % B
    owner_idx = jnp.arange(S, dtype=jnp.int32)[None, :, None]
    global_row = (level_idx * S + owner_idx) * B + within
    flat_rows = global_row.reshape(S, rows_dev)
    source_keys = jax.random.split(key_source, S)
    shuffle = jax.vmap(lambda sub_key: jax.random.permutation(sub_key, rows_dev))(source_keys)
    placed = jnp.take_along_axis(flat_rows, shuffle, axis=1)
    return placed.reshape(NROWS).astype(jnp.int32)


def draw_diag_inverse(key, part):
    key_noise, key_diag = jax.random.split(key)
    shape = (NLEV, S, B, B)
    row_idx = lax.broadcasted_iota(jnp.int32, shape, 2)
    col_idx = lax.broadcasted_iota(jnp.int32, shape, 3)
    noise = jax.random.normal(key_noise, shape, jnp.float32) * (0.5 / math.sqrt(B))
    diagonal = jax.random.uniform(key_diag, shape, jnp.float32, 0.6, 1.4)
    values = jnp.where(row_idx > col_idx, noise, jnp.where(row_idx == col_idx, diagonal, 0.0))
    return values.astype(jnp.bfloat16)


def with_ends(values, stream_key, least, high):
    place = [jax.random.randint(jax.random.fold_in(stream_key, axis), (), 0, length) for axis, length in enumerate(values.shape)]
    widest = values.shape.index(max(values.shape))
    neighbour = place[:widest] + [(place[widest] + 1) % values.shape[widest]] + place[widest + 1:]
    return values.at[tuple(place)].set(least).at[tuple(neighbour)].set(high)


def levels(key, extent, pieces, smallest, high):
    def one(axis_at, blocks):
        heights = jax.random.uniform(jax.random.fold_in(jax.random.fold_in(key, 6), axis_at), (blocks,), jnp.float32, smallest / len(pieces), high / len(pieces))
        return jnp.repeat(jnp.exp(heights), extent[axis_at] // blocks).reshape((-1,) + (1,) * (len(extent) - axis_at - 1))

    factor_of = one(*pieces[0])
    for cut in pieces[1:]:
        factor_of = factor_of * one(*cut)
    return factor_of


def centred(key, shape, scale, reach, cuts=(), kind=jnp.bfloat16):
    entries = scale * jax.random.normal(key, shape, jnp.float32)
    if cuts:
        entries = entries * levels(key, shape, cuts, -0.22, 0.18)
    return jnp.clip(entries, -reach, reach).astype(kind)


def setup_inputs(seed: int = 0) -> dict:
    keys = jax.random.split(jax.random.key(seed), 6)
    rhs_rows = centred(keys[0], (NROWS, NRHS), 1.0, 6.0, ((0, 32),), jnp.float32)
    dest_row = draw_dest_row(jax.random.fold_in(keys[5], 71), 0)
    diag_inverse = draw_diag_inverse(jax.random.fold_in(keys[5], 71), 0)
    lower_blocks = centred(keys[3], (LEVM, OWNERS, HOLDERS, B, HOLDERS, OWNERS, B), (S * B) ** -0.5, 0.09375, ((1, 8), (4, 4)))
    block_mask = with_ends((jax.random.randint(keys[4], (LEVM, OWNERS, HOLDERS, HOLDERS, OWNERS), 0, 2) < 1).astype(jnp.int32), jax.random.fold_in(keys[4], 1), 0, 1)
    return {"rhs_rows": rhs_rows, "dest_row": dest_row, "diag_inverse": diag_inverse, "lower_blocks": lower_blocks, "block_mask": block_mask}


def couple_down(blocks, mask_level, earlier):
    earlier_f = earlier.reshape(OWNERS, HOLDERS, B, NRHS).astype(jnp.float32)

    def one_owner(inputs):
        row_blocks, row_mask = inputs
        weights = row_blocks.astype(jnp.float32) * row_mask[:, None, :, :, None].astype(jnp.float32)
        partials = jnp.einsum('ikcpj,pcjn->ickn', weights, earlier_f)
        partials = lax.optimization_barrier(partials.astype(jnp.bfloat16)).astype(jnp.float32)
        return jnp.sum(partials, axis=1)

    return lax.map(one_owner, (blocks, mask_level)).reshape(S, B, NRHS)


def couple_up(blocks, mask_level, upper):
    upper_f = upper.reshape(OWNERS, HOLDERS, B, NRHS).astype(jnp.float32)

    def one_owner(carry, inputs):
        row_blocks, row_mask, row_upper = inputs
        weights = row_blocks.astype(jnp.float32) * row_mask[:, None, :, :, None].astype(jnp.float32)
        partial_value = jnp.einsum('ikcpj,ikn->pcjn', weights, row_upper)
        partial_value = lax.optimization_barrier(partial_value.astype(jnp.bfloat16)).astype(jnp.float32)
        return carry + partial_value, None

    start_sum = jnp.zeros((OWNERS, HOLDERS, B, NRHS), jnp.float32)
    totals = lax.scan(one_owner, start_sum, (blocks, mask_level, upper_f))[0]
    return totals.reshape(S, B, NRHS)


def reference(rhs_rows, dest_row, diag_inverse, lower_blocks, block_mask):
    ordered = jnp.zeros_like(rhs_rows).at[dest_row].set(rhs_rows).reshape(NLEV, S, B, NRHS)
    solved = []
    for level_idx in range(NLEV):
        if level_idx == 0:
            residual = ordered[0].astype(jnp.bfloat16)
        else:
            coupled = couple_down(lower_blocks[level_idx - 1], block_mask[level_idx - 1], solved[level_idx - 1])
            residual = (ordered[level_idx] - coupled).astype(jnp.bfloat16)
        product = jnp.einsum('qab,qbn->qan', diag_inverse[level_idx].astype(jnp.float32), residual.astype(jnp.float32))
        solved.append(product.astype(jnp.bfloat16))
    solution = [None] * NLEV
    for level_idx in range(NLEV - 1, -1, -1):
        if level_idx == NLEV - 1:
            residual = solved[level_idx]
        else:
            back_coupled = couple_up(lower_blocks[level_idx], block_mask[level_idx], solution[level_idx + 1])
            residual = (solved[level_idx].astype(jnp.float32) - back_coupled).astype(jnp.bfloat16)
        product = jnp.einsum('qba,qbn->qan', diag_inverse[level_idx].astype(jnp.float32), residual.astype(jnp.float32))
        solution[level_idx] = product.astype(jnp.bfloat16)
    return jnp.stack(solution)
```

```python
import functools

import jax
import jax.numpy as jnp
from jax import lax
from jax.experimental import pallas as pl
from jax.experimental.pallas import tpu as pltpu
from jax.sharding import PartitionSpec as P

B = 128
NLEV = 4
LANES = 128
F32 = jnp.float32
BF16 = jnp.bfloat16


def swap(value, axis, distance):
    count = lax.axis_size(axis)
    return lax.ppermute(value, axis, [(i, i ^ distance) for i in range(count)])


def call(body, out_shape, args, scratch=(), flops=0):
    moved = sum(a.size * a.dtype.itemsize for a in args)
    in_specs = [
        pl.BlockSpec(memory_space=pltpu.SMEM if i == 0 else pltpu.VMEM) for i in range(len(args))
    ]
    several = isinstance(out_shape, (list, tuple))
    out_specs = (
        [pl.BlockSpec(memory_space=pltpu.VMEM) for _ in out_shape]
        if several
        else pl.BlockSpec(memory_space=pltpu.VMEM)
    )
    return pl.pallas_call(
        body,
        out_shape=out_shape,
        in_specs=in_specs,
        out_specs=out_specs,
        scratch_shapes=list(scratch),
        compiler_params=pltpu.CompilerParams(vmem_limit_bytes=40 * 1024 * 1024),
        cost_estimate=pl.CostEstimate(flops=flops, bytes_accessed=moved, transcendentals=0),
    )(*args)


def aligned(start, size, step):
    return pl.ds(pl.multiple_of(start * step, step), size)


def pack_body(supernodes, chunk_rows, total_rows, idx_ref, rhs_ref, dest_ref, out_ref):
    local_rows = rhs_ref.shape[0]
    pairs = supernodes // 2
    shards_per_line = LANES // chunk_rows
    me = idx_ref[2]
    dest = dest_ref[...]
    supernode = (dest // B) % supernodes
    level = dest // (supernodes * B)
    within = dest % B
    pair = supernode // 2
    place_high = (level * 2 + supernode % 2).astype(F32)
    place_low = within.astype(F32)
    pair_iota = lax.broadcasted_iota(jnp.int32, (pairs, local_rows), 0)
    member = pair_iota == pair
    member_f = jnp.where(member, 1.0, 0.0)
    before = (
        lax.broadcasted_iota(jnp.int32, (local_rows, local_rows), 0)
        < lax.broadcasted_iota(jnp.int32, (local_rows, local_rows), 1)
    )
    counts = jnp.dot(
        member_f.astype(BF16), jnp.where(before, 1.0, 0.0).astype(BF16), preferred_element_type=F32
    )
    rank = jnp.sum(member_f * counts, axis=0, keepdims=True).astype(jnp.int32)
    slot = pair * chunk_rows + rank
    chosen = lax.broadcasted_iota(jnp.int32, (local_rows, local_rows), 0) == slot
    sorted_rows = jnp.dot(
        jnp.where(chosen, 1.0, 0.0).astype(BF16),
        rhs_ref[...].astype(BF16),
        preferred_element_type=F32,
    )
    tail = total_rows - chunk_rows
    tail_iota = lax.broadcasted_iota(jnp.int32, (pairs * tail, local_rows), 0)
    tail_pair = tail_iota // tail
    tail_row = tail_iota % tail
    tail_value = jnp.where(tail_row == 0, place_high, jnp.where(tail_row == 1, place_low, 0.0))
    tail_value = jnp.where(tail_pair == pair, tail_value, 0.0).astype(BF16)
    lane = rank + (me % shards_per_line) * chunk_rows
    lane_hot = lax.broadcasted_iota(jnp.int32, (LANES, local_rows), 0) == lane
    tails = lax.dot_general(
        tail_value,
        jnp.where(lane_hot, 1.0, 0.0).astype(BF16),
        (((1,), (1,)), ((), ())),
        preferred_element_type=F32,
    )
    half = rhs_ref.shape[1] // 2
    for g in range(pairs):
        rows = sorted_rows[g * chunk_rows : (g + 1) * chunk_rows]
        ending = tails[g * tail : (g + 1) * tail]
        for h in range(2):
            chunk = jnp.concatenate([rows[:, h * half : (h + 1) * half], ending], axis=0)
            out_ref[2 * g + h] = chunk.astype(BF16)


def place_rows(arrived_ref, first_place, place_count, chunk_rows):
    shards = arrived_ref.shape[0]
    shards_per_line = LANES // chunk_rows
    hots = []
    place = lax.broadcasted_iota(jnp.int32, (place_count, LANES), 0) + first_place
    for first in range(0, shards, shards_per_line):
        ending = jnp.zeros((8, LANES), F32)
        for s in range(first, first + shards_per_line):
            ending = ending + arrived_ref[s, chunk_rows:, :].astype(F32)[:8]
        where_to = (ending[0:1] * B + ending[1:2]).astype(jnp.int32)
        hots.append(jnp.where(place == where_to, 1.0, 0.0).astype(BF16))
    hot = jnp.concatenate(hots, axis=1)
    rows = jnp.concatenate(
        [arrived_ref[s].astype(F32)[:chunk_rows] for s in range(shards)], axis=0
    ).astype(BF16)
    return jnp.dot(hot, rows, preferred_element_type=F32)


def first_body(chunk_rows, idx_ref, arrived_ref, own_ref, par_ref, out_ref, residual):
    residual[...] = place_rows(arrived_ref, 0, 2 * B, chunk_rows).astype(BF16)
    apply_diag(idx_ref[1] % 2, residual, own_ref, par_ref, out_ref)


def apply_diag(parity, residual, own_ref, par_ref, out_ref):
    mine, other = aligned(parity, B, B), aligned(1 - parity, B, B)
    out_ref[mine, :] = jnp.dot(
        own_ref[...], residual[mine, :], preferred_element_type=F32
    ).astype(BF16)
    out_ref[other, :] = jnp.dot(
        par_ref[...], residual[other, :], preferred_element_type=F32
    ).astype(BF16)


def rest_body(chunk_rows, idx_ref, arrived_ref, out_ref):
    out_ref[...] = place_rows(arrived_ref, 2 * B, out_ref.shape[0], chunk_rows).astype(BF16)


def down_body(idx_ref, own_ref, par_ref, *refs, rows, pairs):
    pieces, outs, gathered = refs[:rows], refs[rows : rows + pairs], refs[rows + pairs]
    row, col = idx_ref[0], idx_ref[1]
    parity, pair = col % 2, col // 2
    for kk, piece in enumerate(pieces):
        at = aligned(row ^ kk, B, B)
        gathered[parity, at, :] = piece[0:B]
        gathered[1 - parity, at, :] = piece[B : 2 * B]
    for m in list(range(1, pairs)) + [0]:
        at = aligned(pair ^ m, 2 * B, 2 * B)
        total = jnp.dot(own_ref[at, :], gathered[0], preferred_element_type=F32)
        total = total + jnp.dot(par_ref[at, :], gathered[1], preferred_element_type=F32)
        outs[m][...] = total.astype(outs[m].dtype)


def residual_body(idx_ref, rhs_ref, own_ref, par_ref, kept_ref, *refs, last):
    if last:
        arrived, outs, residual, solved = refs[:-3], refs[-3], refs[-2], refs[-1]
    else:
        arrived, solved, residual = refs[:-2], refs[-2], refs[-1]
    coupled = kept_ref[...]
    for ref in arrived:
        coupled = coupled + ref[...].astype(F32)
    residual[...] = (rhs_ref[...].astype(F32) - coupled).astype(BF16)
    parity = idx_ref[1] % 2
    apply_diag(parity, residual, own_ref, par_ref, solved)
    if last:
        for at, factor in ((parity, own_ref), (1 - parity, par_ref)):
            product = lax.dot_general(
                solved[aligned(at, B, B), :],
                factor[...],
                (((0,), (0,)), ((), ())),
                preferred_element_type=F32,
            )
            outs[:, aligned(at, B, B)] = product.astype(BF16)


def up_body(idx_ref, own_ref, par_ref, *refs, rows, pairs):
    pieces, odd_ref, even_ref = refs[:pairs], refs[pairs], refs[pairs + 1]
    gathered, product = refs[pairs + 2], refs[pairs + 3]
    row, col = idx_ref[0], idx_ref[1]
    parity, pair = col % 2, col // 2
    for m, piece in enumerate(pieces):
        gathered[:, aligned(pair ^ m, 2 * B, 2 * B)] = piece[...]
    product[parity] = jnp.dot(gathered[...], own_ref[...], preferred_element_type=F32)
    product[1 - parity] = jnp.dot(gathered[...], par_ref[...], preferred_element_type=F32)
    for kk in range(rows):
        out = odd_ref if kk % 2 else even_ref
        at = aligned(row ^ kk, B, B)
        for cc in range(2):
            out[kk // 2, :, cc * B : (cc + 1) * B] = product[cc, :, at].astype(out.dtype)


def add_body(idx_ref, even_ref, sibling_ref, *outs):
    for k, out in enumerate(outs):
        out[...] = (even_ref[k] + sibling_ref[k].astype(F32)).astype(out.dtype)


def final_body(idx_ref, solved_ref, own_ref, par_ref, kept_ref, *refs):
    arrived, outs, residual = refs[:-2], refs[-2], refs[-1]
    back = kept_ref[...]
    for ref in arrived:
        back = back + ref[...].astype(F32)
    residual[...] = (solved_ref[...].astype(F32) - back).astype(BF16)
    parity = idx_ref[1] % 2
    for at, factor in ((parity, own_ref), (1 - parity, par_ref)):
        lanes = aligned(at, B, B)
        outs[:, lanes] = jnp.dot(
            residual[:, lanes], factor[...], preferred_element_type=F32
        ).astype(BF16)


def per_device(rhs_rows, dest_row, diag_inverse, lower_blocks, block_mask):
    rows = lax.axis_size("row")
    cols = lax.axis_size("col")
    pairs = cols // 2
    supernodes = rows * cols
    local_rows = rhs_rows.shape[0]
    half = rhs_rows.shape[1] // 2
    chunk_rows = 2 * (local_rows // supernodes)
    total_rows = (chunk_rows + 2 + 15) // 16 * 16
    row, col = lax.axis_index("row"), lax.axis_index("col")
    parity = col % 2
    idx = jnp.stack([row, col, row * cols + col]).astype(jnp.int32)

    def shape(dims, dtype=BF16):
        return jax.ShapeDtypeStruct(dims, dtype)

    diag_own = diag_inverse[:, 0]
    diag_par = swap(diag_own, "col", 1)
    own, par = [], []
    for level in range(NLEV - 1):
        tile = lower_blocks[level, 0, :, :, 0]
        mask = block_mask[level, 0, :, 0, :].astype(BF16)
        masked = (tile * mask[:, None, :, None]).reshape(cols * B, rows * B)
        own.append(masked)
        par.append(swap(masked, "col", 1))

    sending = call(
        functools.partial(pack_body, supernodes, chunk_rows, total_rows),
        shape((supernodes, total_rows, half)),
        (idx, rhs_rows, dest_row.reshape(1, local_rows)),
        flops=2 * local_rows * local_rows * 2 * half,
    )
    arrived = lax.all_to_all(sending, ("row", "col"), split_axis=0, concat_axis=0, tiled=True)
    block = (2 * B, half)
    block_t = (half, 2 * B)
    solved = [
        call(
            functools.partial(first_body, chunk_rows),
            shape(block),
            (idx, arrived, diag_own[0], diag_par[0]),
            [pltpu.VMEM(block, BF16)],
        )
    ]
    rest = call(
        functools.partial(rest_body, chunk_rows),
        shape(((NLEV - 1) * 2 * B, half)),
        (idx, arrived),
    )
    upper = None
    for level in range(1, NLEV):
        pieces = [None] * rows
        pieces[0] = solved[-1]
        for kk in range(2, rows, 2):
            pieces[kk] = swap(solved[-1], "row", kk)
        for kk in range(0, rows, 2):
            pieces[kk + 1] = swap(pieces[kk], "row", 1)
        partial_sums = call(
            functools.partial(down_body, rows=rows, pairs=pairs),
            [shape(block, F32 if m == 0 else BF16) for m in range(pairs)],
            (idx, own[level - 1], par[level - 1], *pieces),
            [pltpu.VMEM((2, rows * B, half), BF16)],
            flops=4 * rows * cols * B * B * half,
        )
        passed = [swap(partial_sums[m], "col", 2 * m) for m in range(1, pairs)]
        last = level == NLEV - 1
        result = call(
            functools.partial(residual_body, last=last),
            shape(block_t if last else block),
            (
                idx,
                rest[(level - 1) * 2 * B : level * 2 * B],
                diag_own[level],
                diag_par[level],
                partial_sums[0],
                *passed,
            ),
            [pltpu.VMEM(block, BF16)] * (2 if last else 1),
        )
        if last:
            upper = result
        else:
            solved.append(result)

    solution = [None] * NLEV
    solution[NLEV - 1] = upper
    for level in range(NLEV - 2, -1, -1):
        pieces = [upper] + [swap(upper, "col", 2 * m) for m in range(1, pairs)]
        odd, even = call(
            functools.partial(up_body, rows=rows, pairs=pairs),
            [shape((rows // 2, *block_t)), shape((rows // 2, *block_t), F32)],
            (idx, own[level], par[level], *pieces),
            [pltpu.VMEM((half, cols * B), BF16), pltpu.VMEM((2, half, rows * B), F32)],
            flops=4 * rows * cols * B * B * half,
        )
        sibling = swap(odd, "row", 1)
        sums = call(
            add_body,
            [shape(block_t, F32 if k == 0 else BF16) for k in range(rows // 2)],
            (idx, even, sibling),
        )
        passed = [swap(sums[k], "row", 2 * k) for k in range(1, rows // 2)]
        upper = call(
            final_body,
            shape(block_t),
            (idx, solved[level].T, diag_own[level], diag_par[level], sums[0], *passed),
            [pltpu.VMEM(block_t, BF16)],
        )
        solution[level] = upper

    results = []
    for level in range(NLEV):
        both = solution[level]
        mine = lax.dynamic_slice_in_dim(both, parity * B, B, axis=1).T
        theirs = lax.dynamic_slice_in_dim(both, (1 - parity) * B, B, axis=1).T
        got = swap(theirs, "col", 1)
        results.append(
            jnp.where(
                parity == 0,
                jnp.concatenate([mine, got], axis=1),
                jnp.concatenate([got, mine], axis=1),
            )
        )
    return jnp.stack(results)[:, None]


def solution(mesh):
    in_specs = (
        P(("row", "col"), None),
        P(("row", "col")),
        P(None, ("row", "col"), None, None),
        P(None, "row", None, None, "col", None, None),
        P(None, "row", None, "col", None),
    )
    out_specs = P(None, ("row", "col"), None, None)
    return jax.shard_map(
        per_device, mesh=mesh, in_specs=in_specs, out_specs=out_specs, check_vma=False
    )
```

```python
import functools

import jax
import jax.numpy as jnp
from jax import lax
from jax.experimental import pallas as pl
from jax.experimental.pallas import tpu as pltpu
from jax.sharding import PartitionSpec as P

B = 128
NLEV = 4
LANES = 128
F32 = jnp.float32
BF16 = jnp.bfloat16


def swap(value, axis, distance):
    count = lax.axis_size(axis)
    return lax.ppermute(value, axis, [(i, i ^ distance) for i in range(count)])


def call(body, out_shape, args, scratch=(), flops=0):
    moved = sum(a.size * a.dtype.itemsize for a in args)
    in_specs = [
        pl.BlockSpec(memory_space=pltpu.SMEM if i == 0 else pltpu.VMEM) for i in range(len(args))
    ]
    several = isinstance(out_shape, (list, tuple))
    out_specs = (
        [pl.BlockSpec(memory_space=pltpu.VMEM) for _ in out_shape]
        if several
        else pl.BlockSpec(memory_space=pltpu.VMEM)
    )
    return pl.pallas_call(
        body,
        out_shape=out_shape,
        in_specs=in_specs,
        out_specs=out_specs,
        scratch_shapes=list(scratch),
        compiler_params=pltpu.CompilerParams(vmem_limit_bytes=40 * 1024 * 1024),
        cost_estimate=pl.CostEstimate(flops=flops, bytes_accessed=moved, transcendentals=0),
    )(*args)


def aligned(start, size, step):
    return pl.ds(pl.multiple_of(start * step, step), size)


def pack_body(rows, cols, chunk_rows, total_rows, idx_ref, rhs_ref, dest_ref, out_ref):
    local_rows = rhs_ref.shape[0]
    supernodes = rows * cols
    pairs = supernodes // 2
    shards_per_line = LANES // chunk_rows
    me = idx_ref[2]
    dest = dest_ref[...]
    supernode = (dest // B) % supernodes
    level = dest // (supernodes * B)
    within = dest % B
    owner_row = supernode // cols
    pair = owner_row // 2 * cols + supernode % cols
    place_high = (level * 2 + owner_row % 2).astype(F32)
    place_low = within.astype(F32)
    pair_iota = lax.broadcasted_iota(jnp.int32, (pairs, local_rows), 0)
    member = pair_iota == pair
    member_f = jnp.where(member, 1.0, 0.0)
    before = (
        lax.broadcasted_iota(jnp.int32, (local_rows, local_rows), 0)
        < lax.broadcasted_iota(jnp.int32, (local_rows, local_rows), 1)
    )
    counts = jnp.dot(
        member_f.astype(BF16), jnp.where(before, 1.0, 0.0).astype(BF16), preferred_element_type=F32
    )
    rank = jnp.sum(member_f * counts, axis=0, keepdims=True).astype(jnp.int32)
    slot = pair * chunk_rows + rank
    chosen = lax.broadcasted_iota(jnp.int32, (local_rows, local_rows), 0) == slot
    sorted_rows = jnp.dot(
        jnp.where(chosen, 1.0, 0.0).astype(BF16),
        rhs_ref[...].astype(BF16),
        preferred_element_type=F32,
    )
    tail = total_rows - chunk_rows
    tail_iota = lax.broadcasted_iota(jnp.int32, (pairs * tail, local_rows), 0)
    tail_pair = tail_iota // tail
    tail_row = tail_iota % tail
    tail_value = jnp.where(tail_row == 0, place_high, jnp.where(tail_row == 1, place_low, 0.0))
    tail_value = jnp.where(tail_pair == pair, tail_value, 0.0).astype(BF16)
    lane = rank + (me % shards_per_line) * chunk_rows
    lane_hot = lax.broadcasted_iota(jnp.int32, (LANES, local_rows), 0) == lane
    tails = lax.dot_general(
        tail_value,
        jnp.where(lane_hot, 1.0, 0.0).astype(BF16),
        (((1,), (1,)), ((), ())),
        preferred_element_type=F32,
    )
    half = rhs_ref.shape[1] // 2
    for g in range(pairs):
        chosen_rows = sorted_rows[g * chunk_rows : (g + 1) * chunk_rows]
        ending = tails[g * tail : (g + 1) * tail]
        for h in range(2):
            side = chosen_rows[:, h * half : (h + 1) * half]
            chunk = jnp.concatenate([side, ending], axis=0)
            out_ref[(2 * (g // cols) + h) * cols + g % cols] = chunk.astype(BF16)


def place_rows(arrived_ref, first_place, place_count, chunk_rows):
    shards = arrived_ref.shape[0]
    shards_per_line = LANES // chunk_rows
    hots = []
    place = lax.broadcasted_iota(jnp.int32, (place_count, LANES), 0) + first_place
    for first in range(0, shards, shards_per_line):
        ending = jnp.zeros((8, LANES), F32)
        for s in range(first, first + shards_per_line):
            ending = ending + arrived_ref[s, chunk_rows:, :].astype(F32)[:8]
        where_to = (ending[0:1] * B + ending[1:2]).astype(jnp.int32)
        hots.append(jnp.where(place == where_to, 1.0, 0.0).astype(BF16))
    hot = jnp.concatenate(hots, axis=1)
    rows = jnp.concatenate(
        [arrived_ref[s].astype(F32)[:chunk_rows] for s in range(shards)], axis=0
    ).astype(BF16)
    return lax.dot_general(
        rows, hot, (((0,), (1,)), ((), ())), preferred_element_type=F32
    ).astype(BF16)


def times(left, right):
    return jnp.dot(left, right, preferred_element_type=F32)


def times_t(left, right):
    return lax.dot_general(left, right, (((1,), (1,)), ((), ())), preferred_element_type=F32)


def apply_diag(product, parity, residual, own_ref, par_ref, out_ref):
    for at, factor in ((parity, own_ref), (1 - parity, par_ref)):
        lanes = aligned(at, B, B)
        out_ref[:, lanes] = product(residual[:, lanes], factor[...]).astype(BF16)


def first_body(chunk_rows, idx_ref, arrived_ref, own_ref, par_ref, out_ref, residual):
    residual[...] = place_rows(arrived_ref, 0, 2 * B, chunk_rows)
    apply_diag(times_t, idx_ref[0] % 2, residual, own_ref, par_ref, out_ref)


def rest_body(chunk_rows, idx_ref, arrived_ref, *outs):
    placed = place_rows(arrived_ref, 2 * B, len(outs) * 2 * B, chunk_rows)
    for k, out in enumerate(outs):
        out[...] = placed[:, k * 2 * B : (k + 1) * 2 * B]


def down_body(idx_ref, own_ref, par_ref, *refs, groups, cols):
    pieces, outs = refs[:groups], refs[groups : groups + cols]
    gathered, product = refs[groups + cols :]
    row, col = idx_ref[0], idx_ref[1]
    parity, group = row % 2, row // 2
    for m, piece in enumerate(pieces):
        gathered[:, aligned(group ^ m, 2 * B, 2 * B)] = piece[...]
    product[parity] = times_t(gathered[...], own_ref[...])
    product[1 - parity] = times_t(gathered[...], par_ref[...])
    for m, out in enumerate(outs):
        at = aligned(col ^ m, B, B)
        for rr in range(2):
            out[:, rr * B : (rr + 1) * B] = product[rr, :, at].astype(out.dtype)


def residual_body(idx_ref, rhs_ref, own_ref, par_ref, kept_ref, *refs, last):
    if last:
        arrived, outs, residual, solved = refs[:-3], refs[-3], refs[-2], refs[-1]
    else:
        arrived, solved, residual = refs[:-2], refs[-2], refs[-1]
    coupled = kept_ref[...]
    for ref in arrived:
        coupled = coupled + ref[...].astype(F32)
    residual[...] = (rhs_ref[...].astype(F32) - coupled).astype(BF16)
    parity = idx_ref[0] % 2
    apply_diag(times_t, parity, residual, own_ref, par_ref, solved)
    if last:
        apply_diag(times, parity, solved, own_ref, par_ref, outs)


def up_body(idx_ref, own_ref, par_ref, *refs, groups, cols):
    pieces, outs = refs[:cols], refs[cols : cols + groups]
    gathered, product = refs[cols + groups :]
    row, col = idx_ref[0], idx_ref[1]
    parity, group = row % 2, row // 2
    for m, piece in enumerate(pieces):
        for rr in range(2):
            gathered[rr, :, aligned(col ^ m, B, B)] = piece[:, rr * B : (rr + 1) * B]
    product[...] = times(gathered[parity], own_ref[...]) + times(
        gathered[1 - parity], par_ref[...]
    )
    for m, out in enumerate(outs):
        out[...] = product[:, aligned(group ^ m, 2 * B, 2 * B)].astype(out.dtype)


def final_body(idx_ref, solved_ref, own_ref, par_ref, kept_ref, *refs):
    arrived, outs, residual = refs[:-2], refs[-2], refs[-1]
    back = kept_ref[...]
    for ref in arrived:
        back = back + ref[...].astype(F32)
    residual[...] = (solved_ref[...].astype(F32) - back).astype(BF16)
    apply_diag(times, idx_ref[0] % 2, residual, own_ref, par_ref, outs)


def per_device(rhs_rows, dest_row, diag_inverse, lower_blocks, block_mask):
    rows = lax.axis_size("row")
    cols = lax.axis_size("col")
    groups = rows // 2
    supernodes = rows * cols
    local_rows = rhs_rows.shape[0]
    half = rhs_rows.shape[1] // 2
    chunk_rows = 2 * (local_rows // supernodes)
    total_rows = (chunk_rows + 2 + 15) // 16 * 16
    row, col = lax.axis_index("row"), lax.axis_index("col")
    parity = row % 2
    idx = jnp.stack([row, col, row * cols + col]).astype(jnp.int32)

    def shape(dims, dtype=BF16):
        return jax.ShapeDtypeStruct(dims, dtype)

    diag_own = diag_inverse[:, 0]
    diag_par = swap(diag_own, "row", 1)
    own, par = [], []
    for level in range(NLEV - 1):
        tile = lower_blocks[level, 0, :, :, 0]
        mask = block_mask[level, 0, :, 0, :].astype(BF16)
        masked = (tile * mask[:, None, :, None]).reshape(cols * B, rows * B)
        own.append(masked)
        par.append(swap(masked, "row", 1))

    sending = call(
        functools.partial(pack_body, rows, cols, chunk_rows, total_rows),
        shape((supernodes, total_rows, half)),
        (idx, rhs_rows, dest_row.reshape(1, local_rows)),
        flops=2 * local_rows * local_rows * 2 * half,
    )
    arrived = lax.all_to_all(sending, ("row", "col"), split_axis=0, concat_axis=0, tiled=True)
    block = (half, 2 * B)
    solved = [
        call(
            functools.partial(first_body, chunk_rows),
            shape(block),
            (idx, arrived, diag_own[0], diag_par[0]),
            [pltpu.VMEM(block, BF16)],
        )
    ]
    rest = call(
        functools.partial(rest_body, chunk_rows),
        [shape(block) for _ in range(NLEV - 1)],
        (idx, arrived),
    )
    upper = None
    for level in range(1, NLEV):
        pieces = [solved[-1]] + [swap(solved[-1], "row", 2 * m) for m in range(1, groups)]
        sums = call(
            functools.partial(down_body, groups=groups, cols=cols),
            [shape(block, F32 if m == 0 else BF16) for m in range(cols)],
            (idx, own[level - 1], par[level - 1], *pieces),
            [pltpu.VMEM((half, rows * B), BF16), pltpu.VMEM((2, half, cols * B), F32)],
            flops=4 * rows * cols * B * B * half,
        )
        passed = [swap(sums[m], "col", m) for m in range(1, cols)]
        last = level == NLEV - 1
        result = call(
            functools.partial(residual_body, last=last),
            shape(block),
            (idx, rest[level - 1], diag_own[level], diag_par[level], sums[0], *passed),
            [pltpu.VMEM(block, BF16)] * (2 if last else 1),
        )
        if last:
            upper = result
        else:
            solved.append(result)

    solution = [None] * NLEV
    solution[NLEV - 1] = upper
    for level in range(NLEV - 2, -1, -1):
        pieces = [upper] + [swap(upper, "col", m) for m in range(1, cols)]
        sums = call(
            functools.partial(up_body, groups=groups, cols=cols),
            [shape(block, F32 if m == 0 else BF16) for m in range(groups)],
            (idx, own[level], par[level], *pieces),
            [pltpu.VMEM((2, half, cols * B), BF16), pltpu.VMEM((half, rows * B), F32)],
            flops=4 * rows * cols * B * B * half,
        )
        passed = [swap(sums[m], "row", 2 * m) for m in range(1, groups)]
        upper = call(
            final_body,
            shape(block),
            (idx, solved[level], diag_own[level], diag_par[level], sums[0], *passed),
            [pltpu.VMEM(block, BF16)],
        )
        solution[level] = upper

    results = []
    for level in range(NLEV):
        both = solution[level]
        mine = lax.dynamic_slice_in_dim(both, parity * B, B, axis=1).T
        theirs = lax.dynamic_slice_in_dim(both, (1 - parity) * B, B, axis=1).T
        got = swap(theirs, "row", 1)
        results.append(
            jnp.where(
                parity == 0,
                jnp.concatenate([mine, got], axis=1),
                jnp.concatenate([got, mine], axis=1),
            )
        )
    return jnp.stack(results)[:, None]


def solution(mesh):
    in_specs = (
        P(("row", "col"), None),
        P(("row", "col")),
        P(None, ("row", "col"), None, None),
        P(None, "row", None, None, "col", None, None),
        P(None, "row", None, "col", None),
    )
    out_specs = P(None, ("row", "col"), None, None)
    return jax.shard_map(
        per_device, mesh=mesh, in_specs=in_specs, out_specs=out_specs, check_vma=False
    )
```

```python
import functools

import jax
import jax.numpy as jnp
from jax import lax
from jax.experimental import pallas as pl
from jax.experimental.pallas import tpu as pltpu
from jax.sharding import PartitionSpec as P

B = 128
NLEV = 4
LANES = 128
VMEM_BYTES = 16 * 1024 * 1024
F32 = jnp.float32
BF16 = jnp.bfloat16


def swap(value, axis, distance):
    count = lax.axis_size(axis)
    return lax.ppermute(value, axis, [(i, i ^ distance) for i in range(count)])


def call(body, out_shape, args, scratch=(), flops=0):
    moved = sum(a.size * a.dtype.itemsize for a in args)
    in_specs = [pl.BlockSpec(memory_space=pltpu.VMEM) for _ in args]
    several = isinstance(out_shape, (list, tuple))
    out_specs = (
        [pl.BlockSpec(memory_space=pltpu.VMEM) for _ in out_shape]
        if several
        else pl.BlockSpec(memory_space=pltpu.VMEM)
    )
    return pl.pallas_call(
        body,
        out_shape=out_shape,
        in_specs=in_specs,
        out_specs=out_specs,
        scratch_shapes=list(scratch),
        compiler_params=pltpu.CompilerParams(vmem_limit_bytes=VMEM_BYTES),
        cost_estimate=pl.CostEstimate(flops=flops, bytes_accessed=moved, transcendentals=0),
    )(*args)


def aligned(start, size, step):
    return pl.ds(pl.multiple_of(start * step, step), size)


def fetch_body(own_ref, par_ref, after_ref, own_out, par_out, sems):
    half = own_ref.shape[0] // 2
    copies = []
    for k, (source, target) in enumerate(((own_ref, own_out), (par_ref, par_out))):
        for h in range(2):
            at = pl.ds(h * half, half)
            copies.append(pltpu.make_async_copy(source.at[at], target.at[at], sems.at[2 * k + h]))
    for copy in copies:
        copy.start()
    for copy in copies:
        copy.wait()


def fetch(own, par, after):
    return pl.pallas_call(
        fetch_body,
        out_shape=[pltpu.VMEM(own.shape, own.dtype), pltpu.VMEM(par.shape, par.dtype)],
        in_specs=[pl.BlockSpec(memory_space=pl.ANY)] * 3,
        out_specs=[pl.BlockSpec(memory_space=pltpu.VMEM)] * 2,
        scratch_shapes=[pltpu.SemaphoreType.DMA((4,))],
        compiler_params=pltpu.CompilerParams(vmem_limit_bytes=VMEM_BYTES),
        cost_estimate=pl.CostEstimate(
            flops=0, bytes_accessed=4 * own.size * own.dtype.itemsize, transcendentals=0
        ),
    )(own, par, after)


def pack_body(rows, cols, chunk_rows, total_rows, rhs_ref, dest_ref, out_ref):
    local_rows = rhs_ref.shape[0]
    supernodes = rows * cols
    pairs = supernodes // 2
    shards_per_line = LANES // chunk_rows
    me = lax.axis_index("row") * cols + lax.axis_index("col")
    dest = dest_ref[...]
    supernode = (dest // B) % supernodes
    level = dest // (supernodes * B)
    within = dest % B
    owner_row = supernode // cols
    pair = owner_row // 2 * cols + supernode % cols
    place_high = (level * 2 + owner_row % 2).astype(F32)
    place_low = within.astype(F32)
    pair_iota = lax.broadcasted_iota(jnp.int32, (pairs, local_rows), 0)
    member = pair_iota == pair
    member_f = jnp.where(member, 1.0, 0.0)
    before = (
        lax.broadcasted_iota(jnp.int32, (local_rows, local_rows), 0)
        < lax.broadcasted_iota(jnp.int32, (local_rows, local_rows), 1)
    )
    counts = jnp.dot(
        member_f.astype(BF16), jnp.where(before, 1.0, 0.0).astype(BF16), preferred_element_type=F32
    )
    rank = jnp.sum(member_f * counts, axis=0, keepdims=True).astype(jnp.int32)
    slot = pair * chunk_rows + rank
    chosen = lax.broadcasted_iota(jnp.int32, (local_rows, local_rows), 0) == slot
    sorted_rows = jnp.dot(
        jnp.where(chosen, 1.0, 0.0).astype(BF16),
        rhs_ref[...].astype(BF16),
        preferred_element_type=F32,
    )
    tail = total_rows - chunk_rows
    tail_iota = lax.broadcasted_iota(jnp.int32, (pairs * tail, local_rows), 0)
    tail_pair = tail_iota // tail
    tail_row = tail_iota % tail
    tail_value = jnp.where(tail_row == 0, place_high, jnp.where(tail_row == 1, place_low, 0.0))
    tail_value = jnp.where(tail_pair == pair, tail_value, 0.0).astype(BF16)
    lane = rank + (me % shards_per_line) * chunk_rows
    lane_hot = lax.broadcasted_iota(jnp.int32, (LANES, local_rows), 0) == lane
    tails = lax.dot_general(
        tail_value,
        jnp.where(lane_hot, 1.0, 0.0).astype(BF16),
        (((1,), (1,)), ((), ())),
        preferred_element_type=F32,
    )
    half = rhs_ref.shape[1] // 2
    for g in range(pairs):
        chosen_rows = sorted_rows[g * chunk_rows : (g + 1) * chunk_rows]
        ending = tails[g * tail : (g + 1) * tail]
        for h in range(2):
            side = chosen_rows[:, h * half : (h + 1) * half]
            chunk = jnp.concatenate([side, ending], axis=0)
            out_ref[(2 * (g // cols) + h) * cols + g % cols] = chunk.astype(BF16)


def place_rows(arrived_ref, first_place, place_count, chunk_rows):
    shards = arrived_ref.shape[0]
    shards_per_line = LANES // chunk_rows
    hots = []
    place = lax.broadcasted_iota(jnp.int32, (place_count, LANES), 0) + first_place
    for first in range(0, shards, shards_per_line):
        ending = jnp.zeros((8, LANES), F32)
        for s in range(first, first + shards_per_line):
            ending = ending + arrived_ref[s, chunk_rows:, :].astype(F32)[:8]
        where_to = (ending[0:1] * B + ending[1:2]).astype(jnp.int32)
        hots.append(jnp.where(place == where_to, 1.0, 0.0).astype(BF16))
    hot = jnp.concatenate(hots, axis=1)
    rows = jnp.concatenate(
        [arrived_ref[s].astype(F32)[:chunk_rows] for s in range(shards)], axis=0
    ).astype(BF16)
    return lax.dot_general(
        rows, hot, (((0,), (1,)), ((), ())), preferred_element_type=F32
    ).astype(BF16)


def times(left, right):
    return jnp.dot(left, right, preferred_element_type=F32)


def times_t(left, right):
    return lax.dot_general(left, right, (((1,), (1,)), ((), ())), preferred_element_type=F32)


def apply_diag(product, level, residual, own_ref, par_ref, out_ref):
    parity = lax.axis_index("row") % 2
    for at, factor in ((parity, own_ref), (1 - parity, par_ref)):
        lanes = aligned(at, B, B)
        out_ref[:, lanes] = product(residual[:, lanes], factor[level]).astype(BF16)


def first_body(chunk_rows, arrived_ref, own_ref, par_ref, out_ref, residual):
    residual[...] = place_rows(arrived_ref, 0, 2 * B, chunk_rows)
    apply_diag(times_t, 0, residual, own_ref, par_ref, out_ref)


def rest_body(chunk_rows, arrived_ref, *outs):
    placed = place_rows(arrived_ref, 2 * B, len(outs) * 2 * B, chunk_rows)
    for k, out in enumerate(outs):
        out[...] = placed[:, k * 2 * B : (k + 1) * 2 * B]


def down_body(own_ref, par_ref, *refs, groups, cols):
    pieces, outs = refs[:groups], refs[groups : groups + cols]
    gathered, product = refs[groups + cols :]
    row, col = lax.axis_index("row"), lax.axis_index("col")
    parity, group = row % 2, row // 2
    for m, piece in enumerate(pieces):
        gathered[:, aligned(group ^ m, 2 * B, 2 * B)] = piece[...]
    product[parity] = times_t(gathered[...], own_ref[...])
    product[1 - parity] = times_t(gathered[...], par_ref[...])
    for m, out in enumerate(outs):
        at = aligned(col ^ m, B, B)
        for rr in range(2):
            out[:, rr * B : (rr + 1) * B] = product[rr, :, at].astype(out.dtype)


def residual_body(rhs_ref, own_ref, par_ref, kept_ref, *refs, level):
    last = level == NLEV - 1
    if last:
        arrived, outs, residual, solved = refs[:-3], refs[-3], refs[-2], refs[-1]
    else:
        arrived, solved, residual = refs[:-2], refs[-2], refs[-1]
    coupled = kept_ref[...]
    for ref in arrived:
        coupled = coupled + ref[...].astype(F32)
    residual[...] = (rhs_ref[...].astype(F32) - coupled).astype(BF16)
    apply_diag(times_t, level, residual, own_ref, par_ref, solved)
    if last:
        apply_diag(times, level, solved, own_ref, par_ref, outs)


def up_body(own_ref, par_ref, *refs, groups, cols):
    pieces, outs = refs[:cols], refs[cols : cols + groups]
    gathered, product = refs[cols + groups :]
    row, col = lax.axis_index("row"), lax.axis_index("col")
    parity, group = row % 2, row // 2
    for m, piece in enumerate(pieces):
        for rr in range(2):
            gathered[rr, :, aligned(col ^ m, B, B)] = piece[:, rr * B : (rr + 1) * B]
    product[...] = times(gathered[parity], own_ref[...]) + times(
        gathered[1 - parity], par_ref[...]
    )
    for m, out in enumerate(outs):
        out[...] = product[:, aligned(group ^ m, 2 * B, 2 * B)].astype(out.dtype)


def final_body(solved_ref, own_ref, par_ref, kept_ref, *refs, level):
    arrived, outs, residual = refs[:-2], refs[-2], refs[-1]
    back = kept_ref[...]
    for ref in arrived:
        back = back + ref[...].astype(F32)
    residual[...] = (solved_ref[...].astype(F32) - back).astype(BF16)
    apply_diag(times, level, residual, own_ref, par_ref, outs)


def per_device(rhs_rows, dest_row, diag_inverse, lower_blocks, block_mask):
    rows = lax.axis_size("row")
    cols = lax.axis_size("col")
    groups = rows // 2
    supernodes = rows * cols
    local_rows = rhs_rows.shape[0]
    half = rhs_rows.shape[1] // 2
    chunk_rows = 2 * (local_rows // supernodes)
    total_rows = (chunk_rows + 2 + 15) // 16 * 16
    parity = lax.axis_index("row") % 2

    def shape(dims, dtype=BF16):
        return jax.ShapeDtypeStruct(dims, dtype)

    diag_own = diag_inverse[:, 0]
    diag_par = swap(diag_own, "row", 1)
    own, par = [], []
    for level in range(NLEV - 1):
        tile = lower_blocks[level, 0, :, :, 0]
        mask = block_mask[level, 0, :, 0, :].astype(BF16)
        masked = (tile * mask[:, None, :, None]).reshape(cols * B, rows * B)
        own.append(masked)
        par.append(swap(masked, "row", 1))

    sending = call(
        functools.partial(pack_body, rows, cols, chunk_rows, total_rows),
        shape((supernodes, total_rows, half)),
        (rhs_rows, dest_row.reshape(1, local_rows)),
        flops=2 * local_rows * local_rows * 2 * half,
    )
    arrived = lax.all_to_all(sending, ("row", "col"), split_axis=0, concat_axis=0, tiled=True)
    block = (half, 2 * B)
    solved = [
        call(
            functools.partial(first_body, chunk_rows),
            shape(block),
            (arrived, diag_own, diag_par),
            [pltpu.VMEM(block, BF16)],
        )
    ]
    rest = call(
        functools.partial(rest_body, chunk_rows),
        [shape(block) for _ in range(NLEV - 1)],
        (arrived,),
    )
    upper = None
    for level in range(1, NLEV):
        pieces = [solved[-1]] + [swap(solved[-1], "row", 2 * m) for m in range(1, groups)]
        sums = call(
            functools.partial(down_body, groups=groups, cols=cols),
            [shape(block, F32 if m == 0 else BF16) for m in range(cols)],
            (*fetch(own[level - 1], par[level - 1], solved[-1]), *pieces),
            [pltpu.VMEM((half, rows * B), BF16), pltpu.VMEM((2, half, cols * B), F32)],
            flops=4 * rows * cols * B * B * half,
        )
        passed = [swap(sums[m], "col", m) for m in range(1, cols)]
        last = level == NLEV - 1
        result = call(
            functools.partial(residual_body, level=level),
            shape(block),
            (rest[level - 1], diag_own, diag_par, sums[0], *passed),
            [pltpu.VMEM(block, BF16)] * (2 if last else 1),
        )
        if last:
            upper = result
        else:
            solved.append(result)

    solution = [None] * NLEV
    solution[NLEV - 1] = upper
    for level in range(NLEV - 2, -1, -1):
        pieces = [upper] + [swap(upper, "col", m) for m in range(1, cols)]
        sums = call(
            functools.partial(up_body, groups=groups, cols=cols),
            [shape(block, F32 if m == 0 else BF16) for m in range(groups)],
            (*fetch(own[level], par[level], upper), *pieces),
            [pltpu.VMEM((2, half, cols * B), BF16), pltpu.VMEM((half, rows * B), F32)],
            flops=4 * rows * cols * B * B * half,
        )
        passed = [swap(sums[m], "row", 2 * m) for m in range(1, groups)]
        upper = call(
            functools.partial(final_body, level=level),
            shape(block),
            (solved[level], diag_own, diag_par, sums[0], *passed),
            [pltpu.VMEM(block, BF16)],
        )
        solution[level] = upper

    results = []
    for level in range(NLEV):
        both = solution[level]
        mine = lax.dynamic_slice_in_dim(both, parity * B, B, axis=1).T
        theirs = lax.dynamic_slice_in_dim(both, (1 - parity) * B, B, axis=1).T
        got = swap(theirs, "row", 1)
        results.append(
            jnp.where(
                parity == 0,
                jnp.concatenate([mine, got], axis=1),
                jnp.concatenate([got, mine], axis=1),
            )
        )
    return jnp.stack(results)[:, None]


def solution(mesh):
    in_specs = (
        P(("row", "col"), None),
        P(("row", "col")),
        P(None, ("row", "col"), None, None),
        P(None, "row", None, None, "col", None, None),
        P(None, "row", None, "col", None),
    )
    out_specs = P(None, ("row", "col"), None, None)
    return jax.shard_map(
        per_device, mesh=mesh, in_specs=in_specs, out_specs=out_specs, check_vma=False
    )
```

```python
import functools

import jax
import jax.numpy as jnp
from jax import lax
from jax.experimental import pallas as pl
from jax.experimental.pallas import tpu as pltpu
from jax.sharding import PartitionSpec as P

B = 128
NLEV = 4
LANES = 128
VMEM_BYTES = 16 * 1024 * 1024
F32 = jnp.float32
BF16 = jnp.bfloat16


def swap(value, axis, distance):
    count = lax.axis_size(axis)
    return lax.ppermute(value, axis, [(i, i ^ distance) for i in range(count)])


def call(body, out_shape, args, scratch=(), flops=0, space=pltpu.VMEM):
    moved = sum(a.size * a.dtype.itemsize for a in args)
    in_specs = [pl.BlockSpec(memory_space=space) for _ in args]
    several = isinstance(out_shape, (list, tuple))
    out_specs = (
        [pl.BlockSpec(memory_space=pltpu.VMEM) for _ in out_shape]
        if several
        else pl.BlockSpec(memory_space=pltpu.VMEM)
    )
    return pl.pallas_call(
        body,
        out_shape=out_shape,
        in_specs=in_specs,
        out_specs=out_specs,
        scratch_shapes=list(scratch),
        compiler_params=pltpu.CompilerParams(vmem_limit_bytes=VMEM_BYTES),
        cost_estimate=pl.CostEstimate(flops=flops, bytes_accessed=moved, transcendentals=0),
    )(*args)


def aligned(start, size, step):
    return pl.ds(pl.multiple_of(start * step, step), size)


def fetch_body(own_ref, par_ref, after_ref, own_out, par_out, sems):
    half = own_ref.shape[0] // 2
    copies = []
    for k, (source, target) in enumerate(((own_ref, own_out), (par_ref, par_out))):
        for h in range(2):
            at = pl.ds(h * half, half)
            copies.append(pltpu.make_async_copy(source.at[at], target.at[at], sems.at[2 * k + h]))
    for copy in copies:
        copy.start()
    for copy in copies:
        copy.wait()


def fetch(own, par, after):
    return pl.pallas_call(
        fetch_body,
        out_shape=[pltpu.VMEM(own.shape, own.dtype), pltpu.VMEM(par.shape, par.dtype)],
        in_specs=[pl.BlockSpec(memory_space=pl.ANY)] * 3,
        out_specs=[pl.BlockSpec(memory_space=pltpu.VMEM)] * 2,
        scratch_shapes=[pltpu.SemaphoreType.DMA((4,))],
        compiler_params=pltpu.CompilerParams(vmem_limit_bytes=VMEM_BYTES),
        cost_estimate=pl.CostEstimate(
            flops=0, bytes_accessed=4 * own.size * own.dtype.itemsize, transcendentals=0
        ),
    )(own, par, after)


def pack_body(
    rows, cols, chunk_rows, total_rows, rhs_ref, dest_ref, out_ref
):
    local_rows = rhs_ref.shape[0]
    supernodes = rows * cols
    pairs = supernodes // 2
    shards_per_line = LANES // chunk_rows
    me = lax.axis_index("row") * cols + lax.axis_index("col")
    dest = dest_ref[...]
    supernode = (dest // B) % supernodes
    level = dest // (supernodes * B)
    within = dest % B
    owner_row = supernode // cols
    pair = owner_row // 2 * cols + supernode % cols
    place_high = (level * 2 + owner_row % 2).astype(F32)
    place_low = within.astype(F32)
    pair_iota = lax.broadcasted_iota(jnp.int32, (pairs, local_rows), 0)
    member = pair_iota == pair
    member_f = jnp.where(member, 1.0, 0.0)
    before = (
        lax.broadcasted_iota(jnp.int32, (local_rows, local_rows), 0)
        < lax.broadcasted_iota(jnp.int32, (local_rows, local_rows), 1)
    )
    counts = jnp.dot(
        member_f.astype(BF16), jnp.where(before, 1.0, 0.0).astype(BF16), preferred_element_type=F32
    )
    rank = jnp.sum(member_f * counts, axis=0, keepdims=True).astype(jnp.int32)
    slot = pair * chunk_rows + rank
    chosen = lax.broadcasted_iota(jnp.int32, (local_rows, local_rows), 0) == slot
    tail = total_rows - chunk_rows
    tail_iota = lax.broadcasted_iota(jnp.int32, (pairs * tail, local_rows), 0)
    tail_pair = tail_iota // tail
    tail_row = tail_iota % tail
    tail_value = jnp.where(tail_row == 0, place_high, jnp.where(tail_row == 1, place_low, 0.0))
    tail_value = jnp.where(tail_pair == pair, tail_value, 0.0).astype(BF16)
    lane = rank + (me % shards_per_line) * chunk_rows
    lane_hot = lax.broadcasted_iota(jnp.int32, (LANES, local_rows), 0) == lane
    tails = lax.dot_general(
        tail_value,
        jnp.where(lane_hot, 1.0, 0.0).astype(BF16),
        (((1,), (1,)), ((), ())),
        preferred_element_type=F32,
    )
    sorted_rows = jnp.dot(
        jnp.where(chosen, 1.0, 0.0).astype(BF16),
        rhs_ref[...].astype(BF16),
        preferred_element_type=F32,
    )
    half = rhs_ref.shape[1] // 2
    for g in range(pairs):
        chosen_rows = sorted_rows[g * chunk_rows : (g + 1) * chunk_rows]
        ending = tails[g * tail : (g + 1) * tail]
        for h in range(2):
            side = chosen_rows[:, h * half : (h + 1) * half]
            chunk = jnp.concatenate([side, ending], axis=0)
            out_ref[(2 * (g // cols) + h) * cols + g % cols] = chunk.astype(BF16)


def place_rows(arrived_ref, first_place, place_count, chunk_rows):
    shards = arrived_ref.shape[0]
    shards_per_line = LANES // chunk_rows
    hots = []
    place = lax.broadcasted_iota(jnp.int32, (place_count, LANES), 0) + first_place
    for first in range(0, shards, shards_per_line):
        ending = jnp.zeros((8, LANES), F32)
        for s in range(first, first + shards_per_line):
            ending = ending + arrived_ref[s, chunk_rows:, :].astype(F32)[:8]
        where_to = (ending[0:1] * B + ending[1:2]).astype(jnp.int32)
        hots.append(jnp.where(place == where_to, 1.0, 0.0).astype(BF16))
    hot = jnp.concatenate(hots, axis=1)
    rows = jnp.concatenate(
        [arrived_ref[s].astype(F32)[:chunk_rows] for s in range(shards)], axis=0
    ).astype(BF16)
    return lax.dot_general(
        rows, hot, (((0,), (1,)), ((), ())), preferred_element_type=F32
    ).astype(BF16)


def times(left, right):
    return jnp.dot(left, right, preferred_element_type=F32)


def times_t(left, right):
    return lax.dot_general(left, right, (((1,), (1,)), ((), ())), preferred_element_type=F32)


def apply_diag(product, level, residual, own_ref, par_ref, out_ref):
    parity = lax.axis_index("row") % 2
    for at, factor in ((parity, own_ref), (1 - parity, par_ref)):
        lanes = aligned(at, B, B)
        out_ref[:, lanes] = product(residual[:, lanes], factor[level]).astype(BF16)


def first_body(chunk_rows, arrived_ref, own_ref, par_ref, out_ref, residual):
    residual[...] = place_rows(arrived_ref, 0, 2 * B, chunk_rows)
    apply_diag(times_t, 0, residual, own_ref, par_ref, out_ref)


def rest_body(chunk_rows, arrived_ref, *outs):
    placed = place_rows(arrived_ref, 2 * B, len(outs) * 2 * B, chunk_rows)
    for k, out in enumerate(outs):
        out[...] = placed[:, k * 2 * B : (k + 1) * 2 * B]


def down_body(own_ref, par_ref, *refs, groups, cols):
    pieces, outs = refs[:groups], refs[groups : groups + cols]
    gathered, product = refs[groups + cols :]
    row, col = lax.axis_index("row"), lax.axis_index("col")
    parity, group = row % 2, row // 2
    for m, piece in enumerate(pieces):
        gathered[:, aligned(group ^ m, 2 * B, 2 * B)] = piece[...]
    product[parity] = times_t(gathered[...], own_ref[...])
    product[1 - parity] = times_t(gathered[...], par_ref[...])
    for m, out in enumerate(outs):
        at = aligned(col ^ m, B, B)
        for rr in range(2):
            out[:, rr * B : (rr + 1) * B] = product[rr, :, at].astype(out.dtype)


def split_off(block_ref, theirs_ref):
    theirs_ref[...] = block_ref[:, aligned(1 - lax.axis_index("row") % 2, B, B)]


def finish_body(*refs):
    blocks, others, out_ref = refs[:NLEV], refs[NLEV : 2 * NLEV], refs[2 * NLEV]
    parity = lax.axis_index("row") % 2
    mine, other = aligned(parity, B, B), aligned(1 - parity, B, B)
    for level in range(NLEV):
        out_ref[level, 0, :, mine] = blocks[level][:, mine].T
        out_ref[level, 0, :, other] = others[level][...].T


def residual_body(rhs_ref, own_ref, par_ref, kept_ref, *refs, level):
    last = level == NLEV - 1
    if last:
        arrived, outs, theirs, residual, solved = refs[:-4], *refs[-4:]
    else:
        arrived, solved, residual = refs[:-2], refs[-2], refs[-1]
    coupled = kept_ref[...]
    for ref in arrived:
        coupled = coupled + ref[...].astype(F32)
    residual[...] = (rhs_ref[...].astype(F32) - coupled).astype(BF16)
    apply_diag(times_t, level, residual, own_ref, par_ref, solved)
    if last:
        apply_diag(times, level, solved, own_ref, par_ref, outs)
        split_off(outs, theirs)


def up_body(own_ref, par_ref, *refs, groups, cols):
    pieces, outs = refs[:cols], refs[cols : cols + groups]
    gathered, product = refs[cols + groups :]
    row, col = lax.axis_index("row"), lax.axis_index("col")
    parity, group = row % 2, row // 2
    for m, piece in enumerate(pieces):
        for rr in range(2):
            gathered[rr, :, aligned(col ^ m, B, B)] = piece[:, rr * B : (rr + 1) * B]
    product[...] = times(gathered[parity], own_ref[...]) + times(
        gathered[1 - parity], par_ref[...]
    )
    for m, out in enumerate(outs):
        out[...] = product[:, aligned(group ^ m, 2 * B, 2 * B)].astype(out.dtype)


def final_body(solved_ref, own_ref, par_ref, kept_ref, *refs, level):
    arrived, outs, theirs, residual = refs[:-3], *refs[-3:]
    back = kept_ref[...]
    for ref in arrived:
        back = back + ref[...].astype(F32)
    residual[...] = (solved_ref[...].astype(F32) - back).astype(BF16)
    apply_diag(times, level, residual, own_ref, par_ref, outs)
    split_off(outs, theirs)


def per_device(rhs_rows, dest_row, diag_inverse, lower_blocks, block_mask):
    rows = lax.axis_size("row")
    cols = lax.axis_size("col")
    groups = rows // 2
    supernodes = rows * cols
    local_rows = rhs_rows.shape[0]
    half = rhs_rows.shape[1] // 2
    chunk_rows = 2 * (local_rows // supernodes)
    total_rows = (chunk_rows + 2 + 7) // 8 * 8

    def shape(dims, dtype=BF16):
        return jax.ShapeDtypeStruct(dims, dtype)

    diag_own = diag_inverse[:, 0]
    diag_par = swap(diag_own, "row", 1)
    own, par = [], [None] * (NLEV - 1)
    for level in range(NLEV - 1):
        tile = lower_blocks[level, 0, :, :, 0]
        mask = block_mask[level, 0, :, 0, :].astype(BF16)
        masked = (tile * mask[:, None, :, None]).reshape(cols * B, rows * B)
        own.append(masked)

    sending = call(
        functools.partial(pack_body, rows, cols, chunk_rows, total_rows),
        shape((supernodes, total_rows, half)),
        (rhs_rows, dest_row.reshape(1, local_rows)),
        flops=2 * local_rows * local_rows * 2 * half,
    )
    arrived = lax.all_to_all(sending, ("row", "col"), split_axis=0, concat_axis=0, tiled=True)
    block = (half, 2 * B)
    solved = [
        call(
            functools.partial(first_body, chunk_rows),
            shape(block),
            (arrived, diag_own, diag_par),
            [pltpu.VMEM(block, BF16)],
        )
    ]
    rest = call(
        functools.partial(rest_body, chunk_rows),
        [shape(block) for _ in range(NLEV - 1)],
        (arrived,),
    )
    upper = None
    for level in range(1, NLEV):
        if level == 1:
            own[0], _ = lax.optimization_barrier((own[0], solved[0]))
            par[0] = swap(own[0], "row", 1)
        if level < NLEV - 1:
            own[level], _ = lax.optimization_barrier((own[level], solved[-1]))
            par[level] = swap(own[level], "row", 1)
        pieces = [solved[-1]] + [swap(solved[-1], "row", 2 * m) for m in range(1, groups)]
        sums = call(
            functools.partial(down_body, groups=groups, cols=cols),
            [shape(block, F32 if m == 0 else BF16) for m in range(cols)],
            (*fetch(own[level - 1], par[level - 1], solved[-1]), *pieces),
            [pltpu.VMEM((half, rows * B), BF16), pltpu.VMEM((2, half, cols * B), F32)],
            flops=4 * rows * cols * B * B * half,
        )
        passed = [swap(sums[m], "col", m) for m in range(1, cols)]
        last = level == NLEV - 1
        result = call(
            functools.partial(residual_body, level=level),
            [shape(block), shape((half, B))] if last else shape(block),
            (rest[level - 1], diag_own, diag_par, sums[0], *passed),
            [pltpu.VMEM(block, BF16)] * (2 if last else 1),
        )
        if last:
            upper, theirs = result
        else:
            solved.append(result)

    solution, others = [None] * NLEV, [None] * NLEV
    solution[NLEV - 1], others[NLEV - 1] = upper, swap(theirs, "row", 1)
    for level in range(NLEV - 2, -1, -1):
        pieces = [upper] + [swap(upper, "col", m) for m in range(1, cols)]
        sums = call(
            functools.partial(up_body, groups=groups, cols=cols),
            [shape(block, F32 if m == 0 else BF16) for m in range(groups)],
            (*fetch(own[level], par[level], upper), *pieces),
            [pltpu.VMEM((2, half, cols * B), BF16), pltpu.VMEM((half, rows * B), F32)],
            flops=4 * rows * cols * B * B * half,
        )
        passed = [swap(sums[m], "row", 2 * m) for m in range(1, groups)]
        upper, theirs = call(
            functools.partial(final_body, level=level),
            [shape(block), shape((half, B))],
            (solved[level], diag_own, diag_par, sums[0], *passed),
            [pltpu.VMEM(block, BF16)],
        )
        solution[level], others[level] = upper, swap(theirs, "row", 1)

    return call(
        finish_body, shape((NLEV, 1, B, 2 * half)), (*solution, *others)
    )


def solution(mesh):
    in_specs = (
        P(("row", "col"), None),
        P(("row", "col")),
        P(None, ("row", "col"), None, None),
        P(None, "row", None, None, "col", None, None),
        P(None, "row", None, "col", None),
    )
    out_specs = P(None, ("row", "col"), None, None)
    return jax.shard_map(
        per_device, mesh=mesh, in_specs=in_specs, out_specs=out_specs, check_vma=False
    )
```

```python
import functools

import jax
import jax.numpy as jnp
from jax import lax
from jax.experimental import pallas as pl
from jax.experimental.pallas import tpu as pltpu
from jax.sharding import PartitionSpec as P

B = 128
NLEV = 4
LANES = 128
VMEM_BYTES = 16 * 1024 * 1024
F32 = jnp.float32
BF16 = jnp.bfloat16


def swap(value, axis, distance):
    count = lax.axis_size(axis)
    return lax.ppermute(value, axis, [(i, i ^ distance) for i in range(count)])


def z_order(count):
    return [count - 1, *range(1, count - 1)]


def call(body, out_shape, args, scratch=(), flops=0, space=pltpu.VMEM, limit=VMEM_BYTES):
    moved = sum(a.size * a.dtype.itemsize for a in args)
    in_specs = [pl.BlockSpec(memory_space=space) for _ in args]
    several = isinstance(out_shape, (list, tuple))
    out_specs = (
        [pl.BlockSpec(memory_space=pltpu.VMEM) for _ in out_shape]
        if several
        else pl.BlockSpec(memory_space=pltpu.VMEM)
    )
    return pl.pallas_call(
        body,
        out_shape=out_shape,
        in_specs=in_specs,
        out_specs=out_specs,
        scratch_shapes=list(scratch),
        compiler_params=pltpu.CompilerParams(vmem_limit_bytes=limit),
        cost_estimate=pl.CostEstimate(flops=flops, bytes_accessed=moved, transcendentals=0),
    )(*args)


def aligned(start, size, step):
    return pl.ds(pl.multiple_of(start * step, step), size)


def fetch_body(own_ref, par_ref, after_ref, out_ref, sems):
    parity = lax.axis_index("row") % 2
    copies = []
    for i in range(own_ref.shape[0] // B):
        source = pl.ds(i * B, B)
        for k, (ref, rr) in enumerate(((own_ref, parity), (par_ref, 1 - parity))):
            target = aligned(2 * i + rr, B, B)
            copies.append(
                pltpu.make_async_copy(ref.at[source], out_ref.at[target], sems.at[2 * i + k])
            )
    for copy in copies:
        copy.start()
    for copy in copies:
        copy.wait()


def fetch(own, par, after):
    return pl.pallas_call(
        fetch_body,
        out_shape=pltpu.VMEM((2 * own.shape[0], own.shape[1]), own.dtype),
        in_specs=[pl.BlockSpec(memory_space=pl.ANY)] * 3,
        out_specs=pl.BlockSpec(memory_space=pltpu.VMEM),
        scratch_shapes=[pltpu.SemaphoreType.DMA((2 * own.shape[0] // B,))],
        compiler_params=pltpu.CompilerParams(vmem_limit_bytes=VMEM_BYTES),
        cost_estimate=pl.CostEstimate(
            flops=0, bytes_accessed=4 * own.size * own.dtype.itemsize, transcendentals=0
        ),
    )(own, par, after)


def pack_body(
    rows, cols, chunk_rows, total_rows, rhs_hbm, dest_hbm, out_ref, rhs_ref, dest_ref, sems
):
    dest_copy = pltpu.make_async_copy(dest_hbm, dest_ref, sems.at[0])
    rhs_copy = pltpu.make_async_copy(rhs_hbm, rhs_ref, sems.at[1])
    dest_copy.start()
    rhs_copy.start()
    dest_copy.wait()
    local_rows = rhs_ref.shape[0]
    supernodes = rows * cols
    pairs = supernodes // 2
    shards_per_line = LANES // chunk_rows
    me = lax.axis_index("row") * cols + lax.axis_index("col")
    dest = dest_ref[...]
    supernode = (dest // B) % supernodes
    level = dest // (supernodes * B)
    within = dest % B
    owner_row = supernode // cols
    pair = owner_row // 2 * cols + supernode % cols
    place_high = (level * 2 + owner_row % 2).astype(F32)
    place_low = within.astype(F32)
    pair_iota = lax.broadcasted_iota(jnp.int32, (pairs, local_rows), 0)
    member = pair_iota == pair
    member_f = jnp.where(member, 1.0, 0.0)
    before = (
        lax.broadcasted_iota(jnp.int32, (local_rows, local_rows), 0)
        < lax.broadcasted_iota(jnp.int32, (local_rows, local_rows), 1)
    )
    counts = jnp.dot(
        member_f.astype(BF16), jnp.where(before, 1.0, 0.0).astype(BF16), preferred_element_type=F32
    )
    rank = jnp.sum(member_f * counts, axis=0, keepdims=True).astype(jnp.int32)
    slot = pair * chunk_rows + rank
    chosen = lax.broadcasted_iota(jnp.int32, (local_rows, local_rows), 0) == slot
    tail = total_rows - chunk_rows
    tail_iota = lax.broadcasted_iota(jnp.int32, (pairs * tail, local_rows), 0)
    tail_pair = tail_iota // tail
    tail_row = tail_iota % tail
    tail_value = jnp.where(tail_row == 0, place_high, jnp.where(tail_row == 1, place_low, 0.0))
    tail_value = jnp.where(tail_pair == pair, tail_value, 0.0).astype(BF16)
    lane = rank + (me % shards_per_line) * chunk_rows
    lane_hot = lax.broadcasted_iota(jnp.int32, (LANES, local_rows), 0) == lane
    tails = lax.dot_general(
        tail_value,
        jnp.where(lane_hot, 1.0, 0.0).astype(BF16),
        (((1,), (1,)), ((), ())),
        preferred_element_type=F32,
    )
    rhs_copy.wait()
    sorted_rows = jnp.dot(
        jnp.where(chosen, 1.0, 0.0).astype(BF16),
        rhs_ref[...].astype(BF16),
        preferred_element_type=F32,
    )
    half = rhs_ref.shape[1] // 2
    for g in range(pairs):
        chosen_rows = sorted_rows[g * chunk_rows : (g + 1) * chunk_rows]
        ending = tails[g * tail : (g + 1) * tail]
        for h in range(2):
            side = chosen_rows[:, h * half : (h + 1) * half]
            chunk = jnp.concatenate([side, ending], axis=0)
            out_ref[(2 * (g // cols) + h) * cols + g % cols] = chunk.astype(BF16)


def place_rows(arrived_ref, first_place, place_count, chunk_rows):
    shards = arrived_ref.shape[0]
    shards_per_line = LANES // chunk_rows
    hots = []
    place = lax.broadcasted_iota(jnp.int32, (place_count, LANES), 0) + first_place
    for first in range(0, shards, shards_per_line):
        ending = jnp.zeros((8, LANES), F32)
        for s in range(first, first + shards_per_line):
            ending = ending + arrived_ref[s, chunk_rows:, :].astype(F32)[:8]
        where_to = (ending[0:1] * B + ending[1:2]).astype(jnp.int32)
        hots.append(jnp.where(place == where_to, 1.0, 0.0).astype(BF16))
    hot = jnp.concatenate(hots, axis=1)
    rows = jnp.concatenate(
        [arrived_ref[s].astype(F32)[:chunk_rows] for s in range(shards)], axis=0
    ).astype(BF16)
    return lax.dot_general(
        rows, hot, (((0,), (1,)), ((), ())), preferred_element_type=F32
    ).astype(BF16)


def times(left, right):
    return jnp.dot(left, right, preferred_element_type=F32)


def times_t(left, right):
    return lax.dot_general(left, right, (((1,), (1,)), ((), ())), preferred_element_type=F32)


def apply_diag(product, level, residual, own_ref, par_ref, out_ref):
    parity = lax.axis_index("row") % 2
    for at, factor in ((parity, own_ref), (1 - parity, par_ref)):
        lanes = aligned(at, B, B)
        out_ref[:, lanes] = product(residual[:, lanes], factor[level]).astype(BF16)


def first_body(chunk_rows, arrived_ref, own_ref, par_ref, out_ref, residual):
    residual[...] = place_rows(arrived_ref, 0, 2 * B, chunk_rows)
    apply_diag(times_t, 0, residual, own_ref, par_ref, out_ref)


def rest_body(chunk_rows, arrived_ref, *outs):
    placed = place_rows(arrived_ref, 2 * B, len(outs) * 2 * B, chunk_rows)
    for k, out in enumerate(outs):
        out[...] = placed[:, k * 2 * B : (k + 1) * 2 * B]


def gather_pieces(pieces, position, gathered):
    for m, piece in enumerate(pieces):
        gathered[:, aligned(position ^ m, 2 * B, 2 * B)] = piece[...]


def down_body(tile_ref, *refs, groups, distances):
    pieces, outs, gathered = refs[:groups], refs[groups:-1], refs[-1]
    col = lax.axis_index("col")
    gather_pieces(pieces, lax.axis_index("row") // 2, gathered)
    for m, out in zip(distances, outs):
        at = aligned(col ^ m, 2 * B, 2 * B)
        out[...] = times_t(gathered[...], tile_ref[at, :]).astype(out.dtype)


def up_body(tile_ref, *refs, cols, distances):
    pieces, outs, gathered = refs[:cols], refs[cols:-1], refs[-1]
    group = lax.axis_index("row") // 2
    gather_pieces(pieces, lax.axis_index("col"), gathered)
    for m, out in zip(distances, outs):
        at = aligned(group ^ m, 2 * B, 2 * B)
        out[...] = times(gathered[...], tile_ref[:, at]).astype(out.dtype)


def split_off(block_ref, theirs_ref):
    theirs_ref[...] = block_ref[:, aligned(1 - lax.axis_index("row") % 2, B, B)]


def finish_body(*refs):
    blocks, others, out_ref = refs[:NLEV], refs[NLEV : 2 * NLEV], refs[2 * NLEV]
    parity = lax.axis_index("row") % 2
    mine, other = aligned(parity, B, B), aligned(1 - parity, B, B)
    for level in range(NLEV):
        out_ref[level, 0, :, mine] = blocks[level][:, mine].T
        out_ref[level, 0, :, other] = others[level][...].T


def residual_body(rhs_ref, own_ref, par_ref, kept_ref, *refs, level):
    last = level == NLEV - 1
    if last:
        arrived, outs, theirs, residual, solved = refs[:-4], *refs[-4:]
    else:
        arrived, solved, residual = refs[:-2], refs[-2], refs[-1]
    coupled = kept_ref[...]
    for ref in arrived:
        coupled = coupled + ref[...].astype(F32)
    residual[...] = (rhs_ref[...].astype(F32) - coupled).astype(BF16)
    apply_diag(times_t, level, residual, own_ref, par_ref, solved)
    if last:
        apply_diag(times, level, solved, own_ref, par_ref, outs)
        split_off(outs, theirs)


def final_body(solved_ref, own_ref, par_ref, kept_ref, *refs, level):
    arrived, outs, theirs, residual = refs[:-3], *refs[-3:]
    back = kept_ref[...]
    for ref in arrived:
        back = back + ref[...].astype(F32)
    residual[...] = (solved_ref[...].astype(F32) - back).astype(BF16)
    apply_diag(times, level, residual, own_ref, par_ref, outs)
    split_off(outs, theirs)


def per_device(rhs_rows, dest_row, diag_inverse, lower_blocks, block_mask):
    rows = lax.axis_size("row")
    cols = lax.axis_size("col")
    groups = rows // 2
    supernodes = rows * cols
    local_rows = rhs_rows.shape[0]
    half = rhs_rows.shape[1] // 2
    chunk_rows = 2 * (local_rows // supernodes)
    total_rows = (chunk_rows + 2 + 7) // 8 * 8

    def shape(dims, dtype=BF16):
        return jax.ShapeDtypeStruct(dims, dtype)

    diag_own = diag_inverse[:, 0]
    diag_par = swap(diag_own, "row", 1)
    own, par = [], [None] * (NLEV - 1)
    for level in range(NLEV - 1):
        tile = lower_blocks[level, 0, :, :, 0]
        mask = block_mask[level, 0, :, 0, :].astype(BF16)
        masked = (tile * mask[:, None, :, None]).reshape(cols * B, rows * B)
        own.append(masked)

    sending = call(
        functools.partial(pack_body, rows, cols, chunk_rows, total_rows),
        shape((supernodes, total_rows, half)),
        (rhs_rows, dest_row.reshape(1, local_rows)),
        [
            pltpu.VMEM(rhs_rows.shape, F32),
            pltpu.VMEM((1, local_rows), jnp.int32),
            pltpu.SemaphoreType.DMA((2,)),
        ],
        space=pl.ANY,
        limit=60 * 1024 * 1024,
        flops=2 * local_rows * local_rows * 2 * half,
    )
    arrived = lax.all_to_all(sending, ("row", "col"), split_axis=0, concat_axis=0, tiled=True)
    block = (half, 2 * B)
    solved = [
        call(
            functools.partial(first_body, chunk_rows),
            shape(block),
            (arrived, diag_own, diag_par),
            [pltpu.VMEM(block, BF16)],
        )
    ]
    rest = call(
        functools.partial(rest_body, chunk_rows),
        [shape(block) for _ in range(NLEV - 1)],
        (arrived,),
    )
    upper = None
    for level in range(1, NLEV):
        if level == 1:
            own[0], _ = lax.optimization_barrier((own[0], solved[0]))
            par[0] = swap(own[0], "row", 1)
        if level < NLEV - 1:
            own[level], _ = lax.optimization_barrier((own[level], solved[-1]))
            par[level] = swap(own[level], "row", 1)
        pieces = [solved[-1]] + [swap(solved[-1], "row", 2 * m) for m in range(1, groups)]
        tiles = fetch(own[level - 1], par[level - 1], solved[-1])
        far = list(range(1, cols))
        sums = [
            call(
                functools.partial(down_body, groups=groups, distances=distances),
                [shape(block, F32 if m == 0 else BF16) for m in distances],
                (tiles, *pieces),
                [pltpu.VMEM((half, rows * B), BF16)],
                flops=4 * rows * B * B * half * len(distances),
            )
            for distances in (far, [0])
        ]
        sums = [*sums[1], *sums[0]]
        passed = [swap(sums[m], "col", m) for m in z_order(cols)]
        last = level == NLEV - 1
        result = call(
            functools.partial(residual_body, level=level),
            [shape(block), shape((half, B))] if last else shape(block),
            (rest[level - 1], diag_own, diag_par, sums[0], *passed),
            [pltpu.VMEM(block, BF16)] * (2 if last else 1),
        )
        if last:
            upper, theirs = result
        else:
            solved.append(result)

    solution, others = [None] * NLEV, [None] * NLEV
    solution[NLEV - 1], others[NLEV - 1] = upper, swap(theirs, "row", 1)
    for level in range(NLEV - 2, -1, -1):
        sent = {m: swap(upper, "col", m) for m in reversed(z_order(cols))}
        pieces = [upper] + [sent[m] for m in range(1, cols)]
        tiles = fetch(own[level], par[level], upper)
        far = list(range(1, groups))
        sums = [
            call(
                functools.partial(up_body, cols=cols, distances=distances),
                [shape(block, F32 if m == 0 else BF16) for m in distances],
                (tiles, *pieces),
                [pltpu.VMEM((half, 2 * cols * B), BF16)],
                flops=4 * cols * B * B * half * len(distances),
            )
            for distances in (far, [0])
        ]
        sums = [*sums[1], *sums[0]]
        passed = [swap(sums[m], "row", 2 * m) for m in range(groups - 1, 0, -1)]
        upper, theirs = call(
            functools.partial(final_body, level=level),
            [shape(block), shape((half, B))],
            (solved[level], diag_own, diag_par, sums[0], *passed),
            [pltpu.VMEM(block, BF16)],
        )
        solution[level], others[level] = upper, swap(theirs, "row", 1)

    return call(
        finish_body, shape((NLEV, 1, B, 2 * half)), (*solution, *others)
    )


def solution(mesh):
    in_specs = (
        P(("row", "col"), None),
        P(("row", "col")),
        P(None, ("row", "col"), None, None),
        P(None, "row", None, None, "col", None, None),
        P(None, "row", None, "col", None),
    )
    out_specs = P(None, ("row", "col"), None, None)
    return jax.shard_map(
        per_device, mesh=mesh, in_specs=in_specs, out_specs=out_specs, check_vma=False
    )
```

```python
import functools

import jax
import jax.numpy as jnp
from jax import lax
from jax.experimental import pallas as pl
from jax.experimental.pallas import tpu as pltpu
from jax.sharding import PartitionSpec as P

B = 128
NLEV = 4
LANES = 128
ROW_ORDER = (3, 1, 2)
COL_ORDER = (3, 1, 2)
VMEM_BYTES = 16 * 1024 * 1024
F32 = jnp.float32
BF16 = jnp.bfloat16


def swap(value, axis, distance):
    count = lax.axis_size(axis)
    return lax.ppermute(value, axis, [(i, i ^ distance) for i in range(count)])


def issue_order(count, first):
    ahead = [m for m in first if m < count]
    return ahead + [m for m in range(count - 1, 0, -1) if m not in ahead]


def call(body, out_shape, args, scratch=(), flops=0, space=pltpu.VMEM, limit=VMEM_BYTES):
    moved = sum(a.size * a.dtype.itemsize for a in args)
    in_specs = [pl.BlockSpec(memory_space=space) for _ in args]
    several = isinstance(out_shape, (list, tuple))
    out_specs = (
        [pl.BlockSpec(memory_space=pltpu.VMEM) for _ in out_shape]
        if several
        else pl.BlockSpec(memory_space=pltpu.VMEM)
    )
    return pl.pallas_call(
        body,
        out_shape=out_shape,
        in_specs=in_specs,
        out_specs=out_specs,
        scratch_shapes=list(scratch),
        compiler_params=pltpu.CompilerParams(vmem_limit_bytes=limit),
        cost_estimate=pl.CostEstimate(flops=flops, bytes_accessed=moved, transcendentals=0),
    )(*args)


def aligned(start, size, step):
    return pl.ds(pl.multiple_of(start * step, step), size)


def fetch_body(own_ref, par_ref, after_ref, out_ref, sems):
    parity = lax.axis_index("row") % 2
    copies = []
    for i in range(own_ref.shape[0] // B):
        source = pl.ds(i * B, B)
        for k, (ref, rr) in enumerate(((own_ref, parity), (par_ref, 1 - parity))):
            target = aligned(2 * i + rr, B, B)
            copies.append(
                pltpu.make_async_copy(ref.at[source], out_ref.at[target], sems.at[2 * i + k])
            )
    for copy in copies:
        copy.start()
    for copy in copies:
        copy.wait()


def fetch(own, par, after):
    return pl.pallas_call(
        fetch_body,
        out_shape=pltpu.VMEM((2 * own.shape[0], own.shape[1]), own.dtype),
        in_specs=[pl.BlockSpec(memory_space=pl.ANY)] * 3,
        out_specs=pl.BlockSpec(memory_space=pltpu.VMEM),
        scratch_shapes=[pltpu.SemaphoreType.DMA((2 * own.shape[0] // B,))],
        compiler_params=pltpu.CompilerParams(vmem_limit_bytes=VMEM_BYTES),
        cost_estimate=pl.CostEstimate(
            flops=0, bytes_accessed=4 * own.size * own.dtype.itemsize, transcendentals=0
        ),
    )(own, par, after)


def fetch_turned_body(own_ref, par_ref, after_ref, out_ref):
    parity = lax.axis_index("row") % 2
    for i in range(own_ref.shape[0] // B):
        source = pl.ds(i * B, B)
        for ref, rr in ((own_ref, parity), (par_ref, 1 - parity)):
            out_ref[:, aligned(2 * i + rr, B, B)] = ref[source, :].T


def fetch_turned(own, par, after):
    return pl.pallas_call(
        fetch_turned_body,
        out_shape=pltpu.VMEM((own.shape[1], 2 * own.shape[0]), own.dtype),
        in_specs=[pl.BlockSpec(memory_space=pltpu.VMEM)] * 2 + [pl.BlockSpec(memory_space=pl.ANY)],
        out_specs=pl.BlockSpec(memory_space=pltpu.VMEM),
        compiler_params=pltpu.CompilerParams(vmem_limit_bytes=VMEM_BYTES),
        cost_estimate=pl.CostEstimate(
            flops=0, bytes_accessed=4 * own.size * own.dtype.itemsize, transcendentals=0
        ),
    )(own, par, after)


def pack_body(
    rows, cols, chunk_rows, total_rows, rhs_hbm, dest_hbm, out_ref, rhs_ref, dest_ref, sems
):
    dest_copy = pltpu.make_async_copy(dest_hbm, dest_ref, sems.at[0])
    rhs_copy = pltpu.make_async_copy(rhs_hbm, rhs_ref, sems.at[1])
    dest_copy.start()
    rhs_copy.start()
    local_rows = rhs_ref.shape[0]
    before = (
        lax.broadcasted_iota(jnp.int32, (local_rows, local_rows), 0)
        < lax.broadcasted_iota(jnp.int32, (local_rows, local_rows), 1)
    )
    before = jnp.where(before, 1.0, 0.0).astype(BF16)
    dest_copy.wait()
    supernodes = rows * cols
    pairs = supernodes // 2
    shards_per_line = LANES // chunk_rows
    me = lax.axis_index("row") * cols + lax.axis_index("col")
    dest = dest_ref[...]
    supernode = (dest // B) % supernodes
    level = dest // (supernodes * B)
    within = dest % B
    owner_row = supernode // cols
    pair = owner_row // 2 * cols + supernode % cols
    place_high = (level * 2 + owner_row % 2).astype(F32)
    place_low = within.astype(F32)
    pair_iota = lax.broadcasted_iota(jnp.int32, (pairs, local_rows), 0)
    member = pair_iota == pair
    member_f = jnp.where(member, 1.0, 0.0)
    counts = jnp.dot(member_f.astype(BF16), before, preferred_element_type=F32)
    rank = jnp.sum(member_f * counts, axis=0, keepdims=True).astype(jnp.int32)
    slot = pair * chunk_rows + rank
    chosen = lax.broadcasted_iota(jnp.int32, (local_rows, local_rows), 0) == slot
    tail = total_rows - chunk_rows
    tail_iota = lax.broadcasted_iota(jnp.int32, (pairs * tail, local_rows), 0)
    tail_pair = tail_iota // tail
    tail_row = tail_iota % tail
    tail_value = jnp.where(tail_row == 0, place_high, jnp.where(tail_row == 1, place_low, 0.0))
    tail_value = jnp.where(tail_pair == pair, tail_value, 0.0).astype(BF16)
    lane = rank + (me % shards_per_line) * chunk_rows
    lane_hot = lax.broadcasted_iota(jnp.int32, (LANES, local_rows), 0) == lane
    tails = lax.dot_general(
        tail_value,
        jnp.where(lane_hot, 1.0, 0.0).astype(BF16),
        (((1,), (1,)), ((), ())),
        preferred_element_type=F32,
    )
    rhs_copy.wait()
    sorted_rows = jnp.dot(
        jnp.where(chosen, 1.0, 0.0).astype(BF16),
        rhs_ref[...].astype(BF16),
        preferred_element_type=F32,
    )
    half = rhs_ref.shape[1] // 2
    for g in range(pairs):
        chosen_rows = sorted_rows[g * chunk_rows : (g + 1) * chunk_rows]
        ending = tails[g * tail : (g + 1) * tail]
        for h in range(2):
            side = chosen_rows[:, h * half : (h + 1) * half]
            chunk = jnp.concatenate([side, ending], axis=0)
            out_ref[(2 * (g // cols) + h) * cols + g % cols] = chunk.astype(BF16)


def place_rows(arrived_ref, first_place, place_count, chunk_rows):
    shards = arrived_ref.shape[0]
    shards_per_line = LANES // chunk_rows
    hots = []
    place = lax.broadcasted_iota(jnp.int32, (place_count, LANES), 0) + first_place
    for first in range(0, shards, shards_per_line):
        ending = jnp.zeros((8, LANES), F32)
        for s in range(first, first + shards_per_line):
            ending = ending + arrived_ref[s, chunk_rows:, :].astype(F32)[:8]
        where_to = (ending[0:1] * B + ending[1:2]).astype(jnp.int32)
        hots.append(jnp.where(place == where_to, 1.0, 0.0).astype(BF16))
    hot = jnp.concatenate(hots, axis=1)
    rows = jnp.concatenate(
        [arrived_ref[s].astype(F32)[:chunk_rows] for s in range(shards)], axis=0
    ).astype(BF16)
    return lax.dot_general(
        rows, hot, (((0,), (1,)), ((), ())), preferred_element_type=F32
    ).astype(BF16)


def times(left, right):
    return jnp.dot(left, right, preferred_element_type=F32)


def times_t(left, right):
    return lax.dot_general(left, right, (((1,), (1,)), ((), ())), preferred_element_type=F32)


def apply_diag(product, level, residual, own_ref, par_ref, out_ref):
    parity = lax.axis_index("row") % 2
    for at, factor in ((parity, own_ref), (1 - parity, par_ref)):
        lanes = aligned(at, B, B)
        out_ref[:, lanes] = product(residual[:, lanes], factor[level]).astype(BF16)


def first_body(chunk_rows, arrived_ref, own_ref, par_ref, out_ref, residual):
    residual[...] = place_rows(arrived_ref, 0, 2 * B, chunk_rows)
    apply_diag(times_t, 0, residual, own_ref, par_ref, out_ref)


def rest_body(chunk_rows, arrived_ref, *outs):
    placed = place_rows(arrived_ref, 2 * B, len(outs) * 2 * B, chunk_rows)
    for k, out in enumerate(outs):
        out[...] = placed[:, k * 2 * B : (k + 1) * 2 * B]


def gather_pieces(pieces, position, gathered):
    for m, piece in enumerate(pieces):
        gathered[:, aligned(position ^ m, 2 * B, 2 * B)] = piece[...]


def down_body(tile_ref, *refs, groups, distances):
    pieces, outs, gathered = refs[:groups], refs[groups:-1], refs[-1]
    col = lax.axis_index("col")
    gather_pieces(pieces, lax.axis_index("row") // 2, gathered)
    for m, out in zip(distances, outs):
        at = aligned(col ^ m, 2 * B, 2 * B)
        out[...] = times(gathered[...], tile_ref[:, at]).astype(out.dtype)


def up_body(tile_ref, *refs, cols, distances):
    pieces, outs, gathered = refs[:cols], refs[cols:-1], refs[-1]
    group = lax.axis_index("row") // 2
    gather_pieces(pieces, lax.axis_index("col"), gathered)
    for m, out in zip(distances, outs):
        at = aligned(group ^ m, 2 * B, 2 * B)
        out[...] = times(gathered[...], tile_ref[:, at]).astype(out.dtype)


def split_off(block_ref, theirs_ref):
    theirs_ref[...] = block_ref[:, aligned(1 - lax.axis_index("row") % 2, B, B)]


def finish_body(*refs):
    blocks, others, out_ref = refs[:NLEV], refs[NLEV:-1], refs[-1]
    parity = lax.axis_index("row") % 2
    mine, other = aligned(parity, B, B), aligned(1 - parity, B, B)
    for level in range(NLEV):
        out_ref[level, 0, :, mine] = blocks[level][:, mine].T
        if level:
            out_ref[level, 0, :, other] = others[level - 1][...].T


def last_body(started_ref, other_ref, out_ref, turned, sem):
    turned[...] = other_ref[...].T
    lanes = aligned(1 - lax.axis_index("row") % 2, B, B)
    copy = pltpu.make_async_copy(turned, out_ref.at[0, 0, :, lanes], sem)
    copy.start()
    copy.wait()


def residual_body(rhs_ref, own_ref, par_ref, kept_ref, *refs, level):
    last = level == NLEV - 1
    if last:
        arrived, outs, theirs, residual, solved = refs[:-4], *refs[-4:]
    else:
        arrived, solved, residual = refs[:-2], refs[-2], refs[-1]
    coupled = kept_ref[...]
    for ref in arrived:
        coupled = coupled + ref[...].astype(F32)
    residual[...] = (rhs_ref[...].astype(F32) - coupled).astype(BF16)
    apply_diag(times_t, level, residual, own_ref, par_ref, solved)
    if last:
        apply_diag(times, level, solved, own_ref, par_ref, outs)
        split_off(outs, theirs)


def final_body(solved_ref, own_ref, par_ref, kept_ref, *refs, level):
    arrived, outs, theirs, residual = refs[:-3], *refs[-3:]
    back = kept_ref[...]
    for ref in arrived:
        back = back + ref[...].astype(F32)
    residual[...] = (solved_ref[...].astype(F32) - back).astype(BF16)
    apply_diag(times, level, residual, own_ref, par_ref, outs)
    split_off(outs, theirs)


def per_device(rhs_rows, dest_row, diag_inverse, lower_blocks, block_mask):
    rows = lax.axis_size("row")
    cols = lax.axis_size("col")
    groups = rows // 2
    supernodes = rows * cols
    local_rows = rhs_rows.shape[0]
    half = rhs_rows.shape[1] // 2
    chunk_rows = 2 * (local_rows // supernodes)
    total_rows = (chunk_rows + 2 + 7) // 8 * 8

    def shape(dims, dtype=BF16):
        return jax.ShapeDtypeStruct(dims, dtype)

    diag_own = diag_inverse[:, 0]
    diag_par = swap(diag_own, "row", 1)
    own, par = [], [None] * (NLEV - 1)
    for level in range(NLEV - 1):
        tile = lower_blocks[level, 0, :, :, 0]
        mask = block_mask[level, 0, :, 0, :].astype(BF16)
        masked = (tile * mask[:, None, :, None]).reshape(cols * B, rows * B)
        own.append(masked)

    sending = call(
        functools.partial(pack_body, rows, cols, chunk_rows, total_rows),
        shape((supernodes, total_rows, half)),
        (rhs_rows, dest_row.reshape(1, local_rows)),
        [
            pltpu.VMEM(rhs_rows.shape, F32),
            pltpu.VMEM((1, local_rows), jnp.int32),
            pltpu.SemaphoreType.DMA((2,)),
        ],
        space=pl.ANY,
        limit=60 * 1024 * 1024,
        flops=2 * local_rows * local_rows * 2 * half,
    )
    arrived = lax.all_to_all(sending, ("row", "col"), split_axis=0, concat_axis=0, tiled=True)
    block = (half, 2 * B)
    solved = [
        call(
            functools.partial(first_body, chunk_rows),
            shape(block),
            (arrived, diag_own, diag_par),
            [pltpu.VMEM(block, BF16)],
        )
    ]
    rest = call(
        functools.partial(rest_body, chunk_rows),
        [shape(block) for _ in range(NLEV - 1)],
        (arrived,),
    )
    upper = None
    for level in range(1, NLEV):
        if level == 1:
            own[0], _ = lax.optimization_barrier((own[0], solved[0]))
            par[0] = swap(own[0], "row", 1)
        if level < NLEV - 1:
            own[level], _ = lax.optimization_barrier((own[level], solved[-1]))
            par[level] = swap(own[level], "row", 1)
        sent = {
            m: swap(solved[-1], "row", 2 * m) for m in reversed(issue_order(groups, ROW_ORDER))
        }
        pieces = [solved[-1]] + [sent[m] for m in range(1, groups)]
        tiles = fetch_turned(own[level - 1], par[level - 1], solved[-1])
        far = list(range(1, cols))
        sums = [
            call(
                functools.partial(down_body, groups=groups, distances=distances),
                [shape(block, F32 if m == 0 else BF16) for m in distances],
                (tiles, *pieces),
                [pltpu.VMEM((half, rows * B), BF16)],
                flops=4 * rows * B * B * half * len(distances),
            )
            for distances in (far, [0])
        ]
        sums = [*sums[1], *sums[0]]
        passed = [swap(sums[m], "col", m) for m in issue_order(cols, COL_ORDER)]
        last = level == NLEV - 1
        result = call(
            functools.partial(residual_body, level=level),
            [shape(block), shape((half, B))] if last else shape(block),
            (rest[level - 1], diag_own, diag_par, sums[0], *passed),
            [pltpu.VMEM(block, BF16)] * (2 if last else 1),
        )
        if last:
            upper, theirs = result
        else:
            solved.append(result)

    solution, others = [None] * NLEV, [None] * NLEV
    solution[NLEV - 1], others[NLEV - 1] = upper, swap(theirs, "row", 1)
    for level in range(NLEV - 2, -1, -1):
        sent = {m: swap(upper, "col", m) for m in reversed(issue_order(cols, COL_ORDER))}
        pieces = [upper] + [sent[m] for m in range(1, cols)]
        tiles = fetch(own[level], par[level], upper)
        far = list(range(1, groups))
        sums = [
            call(
                functools.partial(up_body, cols=cols, distances=distances),
                [shape(block, F32 if m == 0 else BF16) for m in distances],
                (tiles, *pieces),
                [pltpu.VMEM((half, 2 * cols * B), BF16)],
                flops=4 * cols * B * B * half * len(distances),
            )
            for distances in (far, [0])
        ]
        sums = [*sums[1], *sums[0]]
        passed = [swap(sums[m], "row", 2 * m) for m in issue_order(groups, ROW_ORDER)]
        upper, theirs = call(
            functools.partial(final_body, level=level),
            [shape(block), shape((half, B))],
            (solved[level], diag_own, diag_par, sums[0], *passed),
            [pltpu.VMEM(block, BF16)],
        )
        solution[level], others[level] = upper, swap(theirs, "row", 1)

    started = call(
        finish_body, shape((NLEV, 1, B, 2 * half)), (*solution, *others[1:])
    )
    return pl.pallas_call(
        last_body,
        out_shape=shape((NLEV, 1, B, 2 * half)),
        in_specs=[pl.BlockSpec(memory_space=pl.ANY), pl.BlockSpec(memory_space=pltpu.VMEM)],
        out_specs=pl.BlockSpec(memory_space=pl.ANY),
        scratch_shapes=[pltpu.VMEM((B, half), BF16), pltpu.SemaphoreType.DMA],
        input_output_aliases={0: 0},
        compiler_params=pltpu.CompilerParams(vmem_limit_bytes=VMEM_BYTES),
    )(started, others[0])


def solution(mesh):
    in_specs = (
        P(("row", "col"), None),
        P(("row", "col")),
        P(None, ("row", "col"), None, None),
        P(None, "row", None, None, "col", None, None),
        P(None, "row", None, "col", None),
    )
    out_specs = P(None, ("row", "col"), None, None)
    return jax.shard_map(
        per_device, mesh=mesh, in_specs=in_specs, out_specs=out_specs, check_vma=False
    )
```

```python
import functools

import jax
import jax.numpy as jnp
from jax import lax
from jax.experimental import pallas as pl
from jax.experimental.pallas import tpu as pltpu
from jax.sharding import PartitionSpec as P

B = 128
NLEV = 4
LANES = 128
ROW_ORDER = (3, 1, 2)
COL_ORDER = (3, 1, 2)
VMEM_BYTES = 16 * 1024 * 1024
F32 = jnp.float32
BF16 = jnp.bfloat16


def swap(value, axis, distance):
    count = lax.axis_size(axis)
    return lax.ppermute(value, axis, [(i, i ^ distance) for i in range(count)])


def issue_order(count, first):
    ahead = [m for m in first if m < count]
    return ahead + [m for m in range(count - 1, 0, -1) if m not in ahead]


def call(body, out_shape, args, scratch=(), flops=0, space=pltpu.VMEM, limit=VMEM_BYTES):
    moved = sum(a.size * a.dtype.itemsize for a in args)
    in_specs = [pl.BlockSpec(memory_space=space) for _ in args]
    several = isinstance(out_shape, (list, tuple))
    out_specs = (
        [pl.BlockSpec(memory_space=pltpu.VMEM) for _ in out_shape]
        if several
        else pl.BlockSpec(memory_space=pltpu.VMEM)
    )
    return pl.pallas_call(
        body,
        out_shape=out_shape,
        in_specs=in_specs,
        out_specs=out_specs,
        scratch_shapes=list(scratch),
        compiler_params=pltpu.CompilerParams(vmem_limit_bytes=limit),
        cost_estimate=pl.CostEstimate(flops=flops, bytes_accessed=moved, transcendentals=0),
    )(*args)


def aligned(start, size, step):
    return pl.ds(pl.multiple_of(start * step, step), size)


def fetch_body(own_ref, par_ref, after_ref, out_ref, sems):
    parity = lax.axis_index("row") % 2
    copies = []
    for i in range(own_ref.shape[0] // B):
        source = pl.ds(i * B, B)
        for k, (ref, rr) in enumerate(((own_ref, parity), (par_ref, 1 - parity))):
            target = aligned(2 * i + rr, B, B)
            copies.append(
                pltpu.make_async_copy(ref.at[source], out_ref.at[target], sems.at[2 * i + k])
            )
    for copy in copies:
        copy.start()
    for copy in copies:
        copy.wait()


def fetch(own, par, after):
    return pl.pallas_call(
        fetch_body,
        out_shape=pltpu.VMEM((2 * own.shape[0], own.shape[1]), own.dtype),
        in_specs=[pl.BlockSpec(memory_space=pl.ANY)] * 3,
        out_specs=pl.BlockSpec(memory_space=pltpu.VMEM),
        scratch_shapes=[pltpu.SemaphoreType.DMA((2 * own.shape[0] // B,))],
        compiler_params=pltpu.CompilerParams(vmem_limit_bytes=VMEM_BYTES),
        cost_estimate=pl.CostEstimate(
            flops=0, bytes_accessed=4 * own.size * own.dtype.itemsize, transcendentals=0
        ),
    )(own, par, after)


def fetch_turned_body(own_ref, par_ref, after_ref, out_ref):
    parity = lax.axis_index("row") % 2
    for i in range(own_ref.shape[0] // B):
        source = pl.ds(i * B, B)
        for ref, rr in ((own_ref, parity), (par_ref, 1 - parity)):
            out_ref[:, aligned(2 * i + rr, B, B)] = ref[source, :].T


def fetch_turned(own, par, after):
    return pl.pallas_call(
        fetch_turned_body,
        out_shape=pltpu.VMEM((own.shape[1], 2 * own.shape[0]), own.dtype),
        in_specs=[pl.BlockSpec(memory_space=pltpu.VMEM)] * 2 + [pl.BlockSpec(memory_space=pl.ANY)],
        out_specs=pl.BlockSpec(memory_space=pltpu.VMEM),
        compiler_params=pltpu.CompilerParams(vmem_limit_bytes=VMEM_BYTES),
        cost_estimate=pl.CostEstimate(
            flops=0, bytes_accessed=4 * own.size * own.dtype.itemsize, transcendentals=0
        ),
    )(own, par, after)


def pack_body(
    rows, cols, chunk_rows, total_rows, rhs_hbm, dest_hbm, out_ref, rhs_ref, dest_ref, sems
):
    dest_copy = pltpu.make_async_copy(dest_hbm, dest_ref, sems.at[0])
    rhs_copy = pltpu.make_async_copy(rhs_hbm, rhs_ref, sems.at[1])
    dest_copy.start()
    rhs_copy.start()
    local_rows = rhs_ref.shape[0]
    before = (
        lax.broadcasted_iota(jnp.int32, (local_rows, local_rows), 0)
        < lax.broadcasted_iota(jnp.int32, (local_rows, local_rows), 1)
    )
    before = jnp.where(before, 1.0, 0.0).astype(BF16)
    dest_copy.wait()
    supernodes = rows * cols
    pairs = supernodes // 2
    shards_per_line = LANES // chunk_rows
    me = lax.axis_index("row") * cols + lax.axis_index("col")
    dest = dest_ref[...]
    supernode = (dest // B) % supernodes
    level = dest // (supernodes * B)
    within = dest % B
    owner_row = supernode // cols
    pair = owner_row // 2 * cols + supernode % cols
    place_high = (level * 2 + owner_row % 2).astype(F32)
    place_low = within.astype(F32)
    pair_iota = lax.broadcasted_iota(jnp.int32, (pairs, local_rows), 0)
    member = pair_iota == pair
    member_f = jnp.where(member, 1.0, 0.0)
    counts = jnp.dot(member_f.astype(BF16), before, preferred_element_type=F32)
    rank = jnp.sum(member_f * counts, axis=0, keepdims=True).astype(jnp.int32)
    slot = pair * chunk_rows + rank
    chosen = lax.broadcasted_iota(jnp.int32, (local_rows, local_rows), 0) == slot
    tail = total_rows - chunk_rows
    tail_iota = lax.broadcasted_iota(jnp.int32, (pairs * tail, local_rows), 0)
    tail_pair = tail_iota // tail
    tail_row = tail_iota % tail
    tail_value = jnp.where(tail_row == 0, place_high, jnp.where(tail_row == 1, place_low, 0.0))
    tail_value = jnp.where(tail_pair == pair, tail_value, 0.0).astype(BF16)
    lane = rank + (me % shards_per_line) * chunk_rows
    lane_hot = lax.broadcasted_iota(jnp.int32, (LANES, local_rows), 0) == lane
    tails = lax.dot_general(
        tail_value,
        jnp.where(lane_hot, 1.0, 0.0).astype(BF16),
        (((1,), (1,)), ((), ())),
        preferred_element_type=F32,
    )
    rhs_copy.wait()
    sorted_rows = jnp.dot(
        jnp.where(chosen, 1.0, 0.0).astype(BF16),
        rhs_ref[...].astype(BF16),
        preferred_element_type=F32,
    )
    half = rhs_ref.shape[1] // 2
    for g in range(pairs):
        chosen_rows = sorted_rows[g * chunk_rows : (g + 1) * chunk_rows]
        ending = tails[g * tail : (g + 1) * tail]
        for h in range(2):
            side = chosen_rows[:, h * half : (h + 1) * half]
            chunk = jnp.concatenate([side, ending], axis=0)
            out_ref[(2 * (g // cols) + h) * cols + g % cols] = chunk.astype(BF16)


def place_rows(arrived_ref, first_place, place_count, chunk_rows):
    shards = arrived_ref.shape[0]
    shards_per_line = LANES // chunk_rows
    hots = []
    place = lax.broadcasted_iota(jnp.int32, (place_count, LANES), 0) + first_place
    for first in range(0, shards, shards_per_line):
        ending = jnp.zeros((8, LANES), F32)
        for s in range(first, first + shards_per_line):
            ending = ending + arrived_ref[s].astype(F32)[chunk_rows : chunk_rows + 8]
        where_to = (ending[0:1] * B + ending[1:2]).astype(jnp.int32)
        hots.append(jnp.where(place == where_to, 1.0, 0.0).astype(BF16))
    hot = jnp.concatenate(hots, axis=1)
    rows = jnp.concatenate(
        [arrived_ref[s].astype(F32)[:chunk_rows] for s in range(shards)], axis=0
    ).astype(BF16)
    return lax.dot_general(
        rows, hot, (((0,), (1,)), ((), ())), preferred_element_type=F32
    ).astype(BF16)


def times(left, right):
    return jnp.dot(left, right, preferred_element_type=F32)


def times_t(left, right):
    return lax.dot_general(left, right, (((1,), (1,)), ((), ())), preferred_element_type=F32)


def apply_diag(product, level, residual, own_ref, par_ref, out_ref):
    parity = lax.axis_index("row") % 2
    for at, factor in ((parity, own_ref), (1 - parity, par_ref)):
        lanes = aligned(at, B, B)
        out_ref[:, lanes] = product(residual[:, lanes], factor[level]).astype(BF16)


def first_body(chunk_rows, arrived_ref, own_ref, par_ref, out_ref, residual):
    residual[...] = place_rows(arrived_ref, 0, 2 * B, chunk_rows)
    apply_diag(times_t, 0, residual, own_ref, par_ref, out_ref)


def rest_body(chunk_rows, arrived_ref, *outs):
    placed = place_rows(arrived_ref, 2 * B, len(outs) * 2 * B, chunk_rows)
    for k, out in enumerate(outs):
        out[...] = placed[:, k * 2 * B : (k + 1) * 2 * B]


def gather_pieces(pieces, position, gathered):
    for m, piece in enumerate(pieces):
        gathered[:, aligned(position ^ m, 2 * B, 2 * B)] = piece[...]


def down_body(tile_ref, *refs, groups, distances):
    pieces, outs, gathered = refs[:groups], refs[groups:-1], refs[-1]
    col = lax.axis_index("col")
    gather_pieces(pieces, lax.axis_index("row") // 2, gathered)
    for m, out in zip(distances, outs):
        at = aligned(col ^ m, 2 * B, 2 * B)
        out[...] = times(gathered[...], tile_ref[:, at]).astype(out.dtype)


def up_body(tile_ref, *refs, cols, distances):
    pieces, outs, gathered = refs[:cols], refs[cols:-1], refs[-1]
    group = lax.axis_index("row") // 2
    gather_pieces(pieces, lax.axis_index("col"), gathered)
    for m, out in zip(distances, outs):
        at = aligned(group ^ m, 2 * B, 2 * B)
        out[...] = times(gathered[...], tile_ref[:, at]).astype(out.dtype)


def split_off(block_ref, theirs_ref):
    theirs_ref[...] = block_ref[:, aligned(1 - lax.axis_index("row") % 2, B, B)]


def finish_body(*refs):
    blocks, others, out_ref = refs[:NLEV], refs[NLEV:-1], refs[-1]
    parity = lax.axis_index("row") % 2
    mine, other = aligned(parity, B, B), aligned(1 - parity, B, B)
    for level in range(NLEV):
        out_ref[level, 0, :, mine] = blocks[level][:, mine].T
        if level:
            out_ref[level, 0, :, other] = others[level - 1][...].T


def last_body(started_ref, other_ref, out_ref, turned, sem):
    turned[...] = other_ref[...].T
    lanes = aligned(1 - lax.axis_index("row") % 2, B, B)
    copy = pltpu.make_async_copy(turned, out_ref.at[0, 0, :, lanes], sem)
    copy.start()
    copy.wait()


def residual_body(rhs_ref, own_ref, par_ref, kept_ref, *refs, level):
    last = level == NLEV - 1
    if last:
        arrived, outs, theirs, residual, solved = refs[:-4], *refs[-4:]
    else:
        arrived, solved, residual = refs[:-2], refs[-2], refs[-1]
    coupled = kept_ref[...]
    for ref in arrived:
        coupled = coupled + ref[...].astype(F32)
    residual[...] = (rhs_ref[...].astype(F32) - coupled).astype(BF16)
    apply_diag(times_t, level, residual, own_ref, par_ref, solved)
    if last:
        apply_diag(times, level, solved, own_ref, par_ref, outs)
        split_off(outs, theirs)


def final_body(solved_ref, own_ref, par_ref, kept_ref, *refs, level):
    arrived, outs, theirs, residual = refs[:-3], *refs[-3:]
    back = kept_ref[...]
    for ref in arrived:
        back = back + ref[...].astype(F32)
    residual[...] = (solved_ref[...].astype(F32) - back).astype(BF16)
    apply_diag(times, level, residual, own_ref, par_ref, outs)
    split_off(outs, theirs)


def per_device(rhs_rows, dest_row, diag_inverse, lower_blocks, block_mask):
    rows = lax.axis_size("row")
    cols = lax.axis_size("col")
    groups = rows // 2
    supernodes = rows * cols
    local_rows = rhs_rows.shape[0]
    half = rhs_rows.shape[1] // 2
    chunk_rows = 2 * (local_rows // supernodes)
    total_rows = (chunk_rows + 2 + 7) // 8 * 8

    def shape(dims, dtype=BF16):
        return jax.ShapeDtypeStruct(dims, dtype)

    diag_own = diag_inverse[:, 0]
    diag_par = swap(diag_own, "row", 1)
    own, par = [], [None] * (NLEV - 1)
    for level in range(NLEV - 1):
        tile = lower_blocks[level, 0, :, :, 0]
        mask = block_mask[level, 0, :, 0, :].astype(BF16)
        masked = (tile * mask[:, None, :, None]).reshape(cols * B, rows * B)
        own.append(masked)

    sending = call(
        functools.partial(pack_body, rows, cols, chunk_rows, total_rows),
        shape((supernodes, total_rows, half)),
        (rhs_rows, dest_row.reshape(1, local_rows)),
        [
            pltpu.VMEM(rhs_rows.shape, F32),
            pltpu.VMEM((1, local_rows), jnp.int32),
            pltpu.SemaphoreType.DMA((2,)),
        ],
        space=pl.ANY,
        limit=60 * 1024 * 1024,
        flops=2 * local_rows * local_rows * 2 * half,
    )
    arrived = lax.all_to_all(sending, ("row", "col"), split_axis=0, concat_axis=0, tiled=True)
    block = (half, 2 * B)
    solved = [
        call(
            functools.partial(first_body, chunk_rows),
            shape(block),
            (arrived, diag_own, diag_par),
            [pltpu.VMEM(block, BF16)],
        )
    ]
    rest = call(
        functools.partial(rest_body, chunk_rows),
        [shape(block) for _ in range(NLEV - 1)],
        (arrived,),
    )
    upper = None
    for level in range(1, NLEV):
        if level == 1:
            own[0], _ = lax.optimization_barrier((own[0], solved[0]))
            par[0] = swap(own[0], "row", 1)
        if level < NLEV - 1:
            own[level], _ = lax.optimization_barrier((own[level], solved[-1]))
            par[level] = swap(own[level], "row", 1)
        sent = {
            m: swap(solved[-1], "row", 2 * m) for m in reversed(issue_order(groups, ROW_ORDER))
        }
        pieces = [solved[-1]] + [sent[m] for m in range(1, groups)]
        tiles = fetch_turned(own[level - 1], par[level - 1], solved[-1])
        far = list(range(1, cols))
        sums = [
            call(
                functools.partial(down_body, groups=groups, distances=distances),
                [shape(block, F32 if m == 0 else BF16) for m in distances],
                (tiles, *pieces),
                [pltpu.VMEM((half, rows * B), BF16)],
                flops=4 * rows * B * B * half * len(distances),
            )
            for distances in (far, [0])
        ]
        sums = [*sums[1], *sums[0]]
        passed = [swap(sums[m], "col", m) for m in issue_order(cols, COL_ORDER)]
        last = level == NLEV - 1
        result = call(
            functools.partial(residual_body, level=level),
            [shape(block), shape((half, B))] if last else shape(block),
            (rest[level - 1], diag_own, diag_par, sums[0], *passed),
            [pltpu.VMEM(block, BF16)] * (2 if last else 1),
        )
        if last:
            upper, theirs = result
        else:
            solved.append(result)

    solution, others = [None] * NLEV, [None] * NLEV
    solution[NLEV - 1], others[NLEV - 1] = upper, swap(theirs, "row", 1)
    for level in range(NLEV - 2, -1, -1):
        sent = {m: swap(upper, "col", m) for m in reversed(issue_order(cols, COL_ORDER))}
        pieces = [upper] + [sent[m] for m in range(1, cols)]
        tiles = fetch(own[level], par[level], upper)
        far = list(range(1, groups))
        sums = [
            call(
                functools.partial(up_body, cols=cols, distances=distances),
                [shape(block, F32 if m == 0 else BF16) for m in distances],
                (tiles, *pieces),
                [pltpu.VMEM((half, 2 * cols * B), BF16)],
                flops=4 * cols * B * B * half * len(distances),
            )
            for distances in (far, [0])
        ]
        sums = [*sums[1], *sums[0]]
        passed = [swap(sums[m], "row", 2 * m) for m in issue_order(groups, ROW_ORDER)]
        upper, theirs = call(
            functools.partial(final_body, level=level),
            [shape(block), shape((half, B))],
            (solved[level], diag_own, diag_par, sums[0], *passed),
            [pltpu.VMEM(block, BF16)],
        )
        solution[level], others[level] = upper, swap(theirs, "row", 1)

    started = call(
        finish_body, shape((NLEV, 1, B, 2 * half)), (*solution, *others[1:])
    )
    return pl.pallas_call(
        last_body,
        out_shape=shape((NLEV, 1, B, 2 * half)),
        in_specs=[pl.BlockSpec(memory_space=pl.ANY), pl.BlockSpec(memory_space=pltpu.VMEM)],
        out_specs=pl.BlockSpec(memory_space=pl.ANY),
        scratch_shapes=[pltpu.VMEM((B, half), BF16), pltpu.SemaphoreType.DMA],
        input_output_aliases={0: 0},
        compiler_params=pltpu.CompilerParams(vmem_limit_bytes=VMEM_BYTES),
    )(started, others[0])


def solution(mesh):
    in_specs = (
        P(("row", "col"), None),
        P(("row", "col")),
        P(None, ("row", "col"), None, None),
        P(None, "row", None, None, "col", None, None),
        P(None, "row", None, "col", None),
    )
    out_specs = P(None, ("row", "col"), None, None)
    return jax.shard_map(
        per_device, mesh=mesh, in_specs=in_specs, out_specs=out_specs, check_vma=False
    )
```

```python
import functools

import jax
import jax.numpy as jnp
from jax import lax
from jax.experimental import pallas as pl
from jax.experimental.pallas import tpu as pltpu
from jax.sharding import PartitionSpec as P

B = 128
NLEV = 4
LANES = 128
ROW_ORDER = (3, 1, 2)
COL_ORDER = (3, 1, 2)
VMEM_BYTES = 16 * 1024 * 1024
F32 = jnp.float32
BF16 = jnp.bfloat16


def swap(value, axis, distance):
    count = lax.axis_size(axis)
    return lax.ppermute(value, axis, [(i, i ^ distance) for i in range(count)])


def issue_order(count, first):
    ahead = [m for m in first if m < count]
    return ahead + [m for m in range(count - 1, 0, -1) if m not in ahead]


def call(body, out_shape, args, scratch=(), flops=0, space=pltpu.VMEM, limit=VMEM_BYTES):
    moved = sum(a.size * a.dtype.itemsize for a in args)
    in_specs = [pl.BlockSpec(memory_space=space) for _ in args]
    several = isinstance(out_shape, (list, tuple))
    out_specs = (
        [pl.BlockSpec(memory_space=pltpu.VMEM) for _ in out_shape]
        if several
        else pl.BlockSpec(memory_space=pltpu.VMEM)
    )
    return pl.pallas_call(
        body,
        out_shape=out_shape,
        in_specs=in_specs,
        out_specs=out_specs,
        scratch_shapes=list(scratch),
        compiler_params=pltpu.CompilerParams(vmem_limit_bytes=limit),
        cost_estimate=pl.CostEstimate(flops=flops, bytes_accessed=moved, transcendentals=0),
    )(*args)


def aligned(start, size, step):
    return pl.ds(pl.multiple_of(start * step, step), size)


def fetch_body(own_ref, par_ref, after_ref, out_ref, sems):
    parity = lax.axis_index("row") % 2
    copies = []
    for i in range(own_ref.shape[0] // B):
        source = pl.ds(i * B, B)
        for k, (ref, rr) in enumerate(((own_ref, parity), (par_ref, 1 - parity))):
            target = aligned(2 * i + rr, B, B)
            copies.append(
                pltpu.make_async_copy(ref.at[source], out_ref.at[target], sems.at[2 * i + k])
            )
    for copy in copies:
        copy.start()
    for copy in copies:
        copy.wait()


def fetch(own, par, after):
    return pl.pallas_call(
        fetch_body,
        out_shape=pltpu.VMEM((2 * own.shape[0], own.shape[1]), own.dtype),
        in_specs=[pl.BlockSpec(memory_space=pl.ANY)] * 3,
        out_specs=pl.BlockSpec(memory_space=pltpu.VMEM),
        scratch_shapes=[pltpu.SemaphoreType.DMA((2 * own.shape[0] // B,))],
        compiler_params=pltpu.CompilerParams(vmem_limit_bytes=VMEM_BYTES),
        cost_estimate=pl.CostEstimate(
            flops=0, bytes_accessed=4 * own.size * own.dtype.itemsize, transcendentals=0
        ),
    )(own, par, after)


def fetch_turned_body(own_ref, par_ref, after_ref, out_ref):
    parity = lax.axis_index("row") % 2
    for i in range(own_ref.shape[0] // B):
        source = pl.ds(i * B, B)
        for ref, rr in ((own_ref, parity), (par_ref, 1 - parity)):
            out_ref[:, aligned(2 * i + rr, B, B)] = ref[source, :].T


def fetch_turned(own, par, after):
    return pl.pallas_call(
        fetch_turned_body,
        out_shape=pltpu.VMEM((own.shape[1], 2 * own.shape[0]), own.dtype),
        in_specs=[pl.BlockSpec(memory_space=pltpu.VMEM)] * 2 + [pl.BlockSpec(memory_space=pl.ANY)],
        out_specs=pl.BlockSpec(memory_space=pltpu.VMEM),
        compiler_params=pltpu.CompilerParams(vmem_limit_bytes=VMEM_BYTES),
        cost_estimate=pl.CostEstimate(
            flops=0, bytes_accessed=4 * own.size * own.dtype.itemsize, transcendentals=0
        ),
    )(own, par, after)


def pack_body(
    rows, cols, chunk_rows, total_rows, rhs_hbm, dest_hbm, out_ref, rhs_ref, dest_ref, sems
):
    dest_copy = pltpu.make_async_copy(dest_hbm, dest_ref, sems.at[0])
    rhs_copy = pltpu.make_async_copy(rhs_hbm, rhs_ref, sems.at[1])
    dest_copy.start()
    rhs_copy.start()
    local_rows = rhs_ref.shape[0]
    before = (
        lax.broadcasted_iota(jnp.int32, (local_rows, local_rows), 0)
        < lax.broadcasted_iota(jnp.int32, (local_rows, local_rows), 1)
    )
    before = jnp.where(before, 1.0, 0.0).astype(BF16)
    dest_copy.wait()
    supernodes = rows * cols
    pairs = supernodes // 2
    shards_per_line = LANES // chunk_rows
    me = lax.axis_index("row") * cols + lax.axis_index("col")
    dest = dest_ref[...]
    supernode = (dest // B) % supernodes
    level = dest // (supernodes * B)
    within = dest % B
    owner_row = supernode // cols
    pair = owner_row // 2 * cols + supernode % cols
    place_high = (level * 2 + owner_row % 2).astype(F32)
    place_low = within.astype(F32)
    pair_iota = lax.broadcasted_iota(jnp.int32, (pairs, local_rows), 0)
    member = pair_iota == pair
    member_f = jnp.where(member, 1.0, 0.0)
    counts = jnp.dot(member_f.astype(BF16), before, preferred_element_type=F32)
    rank = jnp.sum(member_f * counts, axis=0, keepdims=True).astype(jnp.int32)
    slot = pair * chunk_rows + rank
    chosen = lax.broadcasted_iota(jnp.int32, (local_rows, local_rows), 0) == slot
    tail = total_rows - chunk_rows
    tail_iota = lax.broadcasted_iota(jnp.int32, (pairs * tail, local_rows), 0)
    tail_pair = tail_iota // tail
    tail_row = tail_iota % tail
    tail_value = jnp.where(tail_row == 0, place_high, jnp.where(tail_row == 1, place_low, 0.0))
    tail_value = jnp.where(tail_pair == pair, tail_value, 0.0).astype(BF16)
    lane = rank + (me % shards_per_line) * chunk_rows
    lane_hot = lax.broadcasted_iota(jnp.int32, (LANES, local_rows), 0) == lane
    tails = lax.dot_general(
        tail_value,
        jnp.where(lane_hot, 1.0, 0.0).astype(BF16),
        (((1,), (1,)), ((), ())),
        preferred_element_type=F32,
    )
    rhs_copy.wait()
    sorted_rows = jnp.dot(
        jnp.where(chosen, 1.0, 0.0).astype(BF16),
        rhs_ref[...].astype(BF16),
        preferred_element_type=F32,
    )
    half = rhs_ref.shape[1] // 2
    for g in range(pairs):
        chosen_rows = sorted_rows[g * chunk_rows : (g + 1) * chunk_rows]
        ending = tails[g * tail : (g + 1) * tail]
        for h in range(2):
            side = chosen_rows[:, h * half : (h + 1) * half]
            chunk = jnp.concatenate([side, ending], axis=0)
            out_ref[(2 * (g // cols) + h) * cols + g % cols] = chunk.astype(BF16)


def place_rows(arrived_ref, first_place, place_count, chunk_rows):
    shards = arrived_ref.shape[0]
    shards_per_line = LANES // chunk_rows
    hots = []
    place = lax.broadcasted_iota(jnp.int32, (place_count, LANES), 0) + first_place
    for first in range(0, shards, shards_per_line):
        ending = jnp.zeros((8, LANES), F32)
        for s in range(first, first + shards_per_line):
            ending = ending + arrived_ref[s].astype(F32)[chunk_rows : chunk_rows + 8]
        where_to = (ending[0:1] * B + ending[1:2]).astype(jnp.int32)
        hots.append(jnp.where(place == where_to, 1.0, 0.0).astype(BF16))
    hot = jnp.concatenate(hots, axis=1)
    rows = jnp.concatenate(
        [arrived_ref[s].astype(F32)[:chunk_rows] for s in range(shards)], axis=0
    ).astype(BF16)
    return lax.dot_general(
        rows, hot, (((0,), (1,)), ((), ())), preferred_element_type=F32
    ).astype(BF16)


def times(left, right):
    return jnp.dot(left, right, preferred_element_type=F32)


def times_t(left, right):
    return lax.dot_general(left, right, (((1,), (1,)), ((), ())), preferred_element_type=F32)


def apply_diag(product, level, residual, own_ref, par_ref, out_ref):
    parity = lax.axis_index("row") % 2
    for at, factor in ((parity, own_ref), (1 - parity, par_ref)):
        lanes = aligned(at, B, B)
        out_ref[:, lanes] = product(residual[:, lanes], factor[level]).astype(BF16)


def first_body(chunk_rows, arrived_ref, own_ref, par_ref, out_ref, residual):
    residual[...] = place_rows(arrived_ref, 0, 2 * B, chunk_rows)
    apply_diag(times_t, 0, residual, own_ref, par_ref, out_ref)


def rest_body(chunk_rows, arrived_ref, *outs):
    placed = place_rows(arrived_ref, 2 * B, len(outs) * 2 * B, chunk_rows)
    for k, out in enumerate(outs):
        out[...] = placed[:, k * 2 * B : (k + 1) * 2 * B]


def gather_pieces(pieces, position, gathered):
    for m, piece in enumerate(pieces):
        gathered[:, aligned(position ^ m, 2 * B, 2 * B)] = piece[...]


def down_body(tile_ref, *refs, groups, distances):
    pieces, outs, gathered = refs[:groups], refs[groups:-1], refs[-1]
    col = lax.axis_index("col")
    gather_pieces(pieces, lax.axis_index("row") // 2, gathered)
    for m, out in zip(distances, outs):
        at = aligned(col ^ m, 2 * B, 2 * B)
        out[...] = times(gathered[...], tile_ref[:, at]).astype(out.dtype)


def up_body(tile_ref, *refs, cols, distances):
    pieces, outs, gathered = refs[:cols], refs[cols:-1], refs[-1]
    group = lax.axis_index("row") // 2
    gather_pieces(pieces, lax.axis_index("col"), gathered)
    for m, out in zip(distances, outs):
        at = aligned(group ^ m, 2 * B, 2 * B)
        out[...] = times(gathered[...], tile_ref[:, at]).astype(out.dtype)


def split_off(block_ref, theirs_ref):
    theirs_ref[...] = block_ref[:, aligned(1 - lax.axis_index("row") % 2, B, B)]


def finish_body(*refs):
    blocks, others, out_ref = refs[:NLEV], refs[NLEV], refs[-1]
    parity = lax.axis_index("row") % 2
    mine, other = aligned(parity, B, B), aligned(1 - parity, B, B)
    for level in range(NLEV):
        out_ref[level, 0, :, mine] = blocks[level][:, mine].T
        if level:
            out_ref[level, 0, :, other] = others[:, (level - 1) * B : level * B].T


def last_body(started_ref, other_ref, out_ref, turned, sem):
    turned[...] = other_ref[...].T
    lanes = aligned(1 - lax.axis_index("row") % 2, B, B)
    copy = pltpu.make_async_copy(turned, out_ref.at[0, 0, :, lanes], sem)
    copy.start()
    copy.wait()


def residual_body(rhs_ref, own_ref, par_ref, kept_ref, *refs, level):
    last = level == NLEV - 1
    if last:
        arrived, outs, theirs, residual, solved = refs[:-4], *refs[-4:]
    else:
        arrived, solved, residual = refs[:-2], refs[-2], refs[-1]
    coupled = kept_ref[...]
    for ref in arrived:
        coupled = coupled + ref[...].astype(F32)
    residual[...] = (rhs_ref[...].astype(F32) - coupled).astype(BF16)
    apply_diag(times_t, level, residual, own_ref, par_ref, solved)
    if last:
        apply_diag(times, level, solved, own_ref, par_ref, outs)
        split_off(outs, theirs)


def final_body(solved_ref, own_ref, par_ref, kept_ref, *refs, level):
    arrived, outs, theirs, residual = refs[:-3], *refs[-3:]
    back = kept_ref[...]
    for ref in arrived:
        back = back + ref[...].astype(F32)
    residual[...] = (solved_ref[...].astype(F32) - back).astype(BF16)
    apply_diag(times, level, residual, own_ref, par_ref, outs)
    split_off(outs, theirs)


def per_device(rhs_rows, dest_row, diag_inverse, lower_blocks, block_mask):
    rows = lax.axis_size("row")
    cols = lax.axis_size("col")
    groups = rows // 2
    supernodes = rows * cols
    local_rows = rhs_rows.shape[0]
    half = rhs_rows.shape[1] // 2
    chunk_rows = 2 * (local_rows // supernodes)
    total_rows = (chunk_rows + 2 + 7) // 8 * 8

    def shape(dims, dtype=BF16):
        return jax.ShapeDtypeStruct(dims, dtype)

    diag_own = diag_inverse[:, 0]
    diag_par = swap(diag_own, "row", 1)
    own, par = [], [None] * (NLEV - 1)
    for level in range(NLEV - 1):
        tile = lower_blocks[level, 0, :, :, 0]
        mask = block_mask[level, 0, :, 0, :].astype(BF16)
        masked = (tile * mask[:, None, :, None]).reshape(cols * B, rows * B)
        own.append(masked)

    sending = call(
        functools.partial(pack_body, rows, cols, chunk_rows, total_rows),
        shape((supernodes, total_rows, half)),
        (rhs_rows, dest_row.reshape(1, local_rows)),
        [
            pltpu.VMEM(rhs_rows.shape, F32),
            pltpu.VMEM((1, local_rows), jnp.int32),
            pltpu.SemaphoreType.DMA((2,)),
        ],
        space=pl.ANY,
        limit=60 * 1024 * 1024,
        flops=2 * local_rows * local_rows * 2 * half,
    )
    arrived = lax.all_to_all(sending, ("row", "col"), split_axis=0, concat_axis=0, tiled=True)
    block = (half, 2 * B)
    solved = [
        call(
            functools.partial(first_body, chunk_rows),
            shape(block),
            (arrived, diag_own, diag_par),
            [pltpu.VMEM(block, BF16)],
        )
    ]
    rest = call(
        functools.partial(rest_body, chunk_rows),
        [shape(block) for _ in range(NLEV - 1)],
        (arrived,),
    )
    upper = None
    for level in range(1, NLEV):
        if level == 1:
            own[0], _ = lax.optimization_barrier((own[0], solved[0]))
            par[0] = swap(own[0], "row", 1)
        if level < NLEV - 1:
            own[level], _ = lax.optimization_barrier((own[level], solved[-1]))
            par[level] = swap(own[level], "row", 1)
        sent = {
            m: swap(solved[-1], "row", 2 * m) for m in reversed(issue_order(groups, ROW_ORDER))
        }
        pieces = [solved[-1]] + [sent[m] for m in range(1, groups)]
        tiles = fetch_turned(own[level - 1], par[level - 1], solved[-1])
        far = list(range(1, cols))
        sums = [
            call(
                functools.partial(down_body, groups=groups, distances=distances),
                [shape(block, F32 if m == 0 else BF16) for m in distances],
                (tiles, *pieces),
                [pltpu.VMEM((half, rows * B), BF16)],
                flops=4 * rows * B * B * half * len(distances),
            )
            for distances in (far, [0])
        ]
        sums = [*sums[1], *sums[0]]
        passed = [swap(sums[m], "col", m) for m in issue_order(cols, COL_ORDER)]
        last = level == NLEV - 1
        result = call(
            functools.partial(residual_body, level=level),
            [shape(block), shape((half, B))] if last else shape(block),
            (rest[level - 1], diag_own, diag_par, sums[0], *passed),
            [pltpu.VMEM(block, BF16)] * (2 if last else 1),
        )
        if last:
            upper, theirs = result
        else:
            solved.append(result)

    solution, leaving = [None] * NLEV, [None] * NLEV
    solution[NLEV - 1], leaving[NLEV - 1] = upper, theirs
    for level in range(NLEV - 2, -1, -1):
        sent = {m: swap(upper, "col", m) for m in reversed(issue_order(cols, COL_ORDER))}
        pieces = [upper] + [sent[m] for m in range(1, cols)]
        tiles = fetch(own[level], par[level], upper)
        far = list(range(1, groups))
        sums = [
            call(
                functools.partial(up_body, cols=cols, distances=distances),
                [shape(block, F32 if m == 0 else BF16) for m in distances],
                (tiles, *pieces),
                [pltpu.VMEM((half, 2 * cols * B), BF16)],
                flops=4 * cols * B * B * half * len(distances),
            )
            for distances in (far, [0])
        ]
        sums = [*sums[1], *sums[0]]
        passed = [swap(sums[m], "row", 2 * m) for m in issue_order(groups, ROW_ORDER)]
        upper, theirs = call(
            functools.partial(final_body, level=level),
            [shape(block), shape((half, B))],
            (solved[level], diag_own, diag_par, sums[0], *passed),
            [pltpu.VMEM(block, BF16)],
        )
        solution[level], leaving[level] = upper, theirs

    others = swap(jnp.concatenate(leaving[1:], axis=1), "row", 1)
    first_other = swap(leaving[0], "row", 1)
    started = call(finish_body, shape((NLEV, 1, B, 2 * half)), (*solution, others))
    return pl.pallas_call(
        last_body,
        out_shape=shape((NLEV, 1, B, 2 * half)),
        in_specs=[pl.BlockSpec(memory_space=pl.ANY), pl.BlockSpec(memory_space=pltpu.VMEM)],
        out_specs=pl.BlockSpec(memory_space=pl.ANY),
        scratch_shapes=[pltpu.VMEM((B, half), BF16), pltpu.SemaphoreType.DMA],
        input_output_aliases={0: 0},
        compiler_params=pltpu.CompilerParams(vmem_limit_bytes=VMEM_BYTES),
    )(started, first_other)


def solution(mesh):
    in_specs = (
        P(("row", "col"), None),
        P(("row", "col")),
        P(None, ("row", "col"), None, None),
        P(None, "row", None, None, "col", None, None),
        P(None, "row", None, "col", None),
    )
    out_specs = P(None, ("row", "col"), None, None)
    return jax.shard_map(
        per_device, mesh=mesh, in_specs=in_specs, out_specs=out_specs, check_vma=False
    )
```

```python
import functools

import jax
import jax.numpy as jnp
from jax import lax
from jax.experimental import pallas as pl
from jax.experimental.pallas import tpu as pltpu
from jax.sharding import PartitionSpec as P

B = 128
NLEV = 4
LANES = 128
ROW_ORDER = (3, 1, 2)
COL_ORDER = (3, 1, 2)
TURN_ORDER = (2, 3, 1)
VMEM_BYTES = 16 * 1024 * 1024
F32 = jnp.float32
BF16 = jnp.bfloat16


def swap(value, axis, distance):
    count = lax.axis_size(axis)
    return lax.ppermute(value, axis, [(i, i ^ distance) for i in range(count)])


def issue_order(count, first):
    ahead = [m for m in first if m < count]
    return ahead + [m for m in range(count - 1, 0, -1) if m not in ahead]


def call(body, out_shape, args, scratch=(), flops=0, space=pltpu.VMEM, limit=VMEM_BYTES):
    moved = sum(a.size * a.dtype.itemsize for a in args)
    in_specs = [pl.BlockSpec(memory_space=space) for _ in args]
    several = isinstance(out_shape, (list, tuple))
    out_specs = (
        [pl.BlockSpec(memory_space=pltpu.VMEM) for _ in out_shape]
        if several
        else pl.BlockSpec(memory_space=pltpu.VMEM)
    )
    return pl.pallas_call(
        body,
        out_shape=out_shape,
        in_specs=in_specs,
        out_specs=out_specs,
        scratch_shapes=list(scratch),
        compiler_params=pltpu.CompilerParams(vmem_limit_bytes=limit),
        cost_estimate=pl.CostEstimate(flops=flops, bytes_accessed=moved, transcendentals=0),
    )(*args)


def aligned(start, size, step):
    return pl.ds(pl.multiple_of(start * step, step), size)


def fetch_body(own_ref, par_ref, after_ref, out_ref, sems):
    parity = lax.axis_index("row") % 2
    copies = []
    for i in range(own_ref.shape[0] // B):
        source = pl.ds(i * B, B)
        for k, (ref, rr) in enumerate(((own_ref, parity), (par_ref, 1 - parity))):
            target = aligned(2 * i + rr, B, B)
            copies.append(
                pltpu.make_async_copy(ref.at[source], out_ref.at[target], sems.at[2 * i + k])
            )
    for copy in copies:
        copy.start()
    for copy in copies:
        copy.wait()


def fetch(own, par, after):
    return pl.pallas_call(
        fetch_body,
        out_shape=pltpu.VMEM((2 * own.shape[0], own.shape[1]), own.dtype),
        in_specs=[pl.BlockSpec(memory_space=pl.ANY)] * 3,
        out_specs=pl.BlockSpec(memory_space=pltpu.VMEM),
        scratch_shapes=[pltpu.SemaphoreType.DMA((2 * own.shape[0] // B,))],
        compiler_params=pltpu.CompilerParams(vmem_limit_bytes=VMEM_BYTES),
        cost_estimate=pl.CostEstimate(
            flops=0, bytes_accessed=4 * own.size * own.dtype.itemsize, transcendentals=0
        ),
    )(own, par, after)


def fetch_turned_body(own_ref, par_ref, after_ref, out_ref):
    parity = lax.axis_index("row") % 2
    for i in range(own_ref.shape[0] // B):
        source = pl.ds(i * B, B)
        for ref, rr in ((own_ref, parity), (par_ref, 1 - parity)):
            out_ref[:, aligned(2 * i + rr, B, B)] = ref[source, :].T


def fetch_turned(own, par, after):
    return pl.pallas_call(
        fetch_turned_body,
        out_shape=pltpu.VMEM((own.shape[1], 2 * own.shape[0]), own.dtype),
        in_specs=[pl.BlockSpec(memory_space=pltpu.VMEM)] * 2 + [pl.BlockSpec(memory_space=pl.ANY)],
        out_specs=pl.BlockSpec(memory_space=pltpu.VMEM),
        compiler_params=pltpu.CompilerParams(vmem_limit_bytes=VMEM_BYTES),
        cost_estimate=pl.CostEstimate(
            flops=0, bytes_accessed=4 * own.size * own.dtype.itemsize, transcendentals=0
        ),
    )(own, par, after)


def pack_body(
    rows, cols, chunk_rows, total_rows, rhs_hbm, dest_hbm, out_ref, rhs_ref, dest_ref, sems
):
    dest_copy = pltpu.make_async_copy(dest_hbm, dest_ref, sems.at[0])
    rhs_copy = pltpu.make_async_copy(rhs_hbm, rhs_ref, sems.at[1])
    dest_copy.start()
    rhs_copy.start()
    local_rows = rhs_ref.shape[0]
    before = (
        lax.broadcasted_iota(jnp.int32, (local_rows, local_rows), 0)
        < lax.broadcasted_iota(jnp.int32, (local_rows, local_rows), 1)
    )
    before = jnp.where(before, 1.0, 0.0).astype(BF16)
    dest_copy.wait()
    supernodes = rows * cols
    pairs = supernodes // 2
    shards_per_line = LANES // chunk_rows
    me = lax.axis_index("row") * cols + lax.axis_index("col")
    dest = dest_ref[...]
    supernode = (dest // B) % supernodes
    level = dest // (supernodes * B)
    within = dest % B
    owner_row = supernode // cols
    pair = owner_row // 2 * cols + supernode % cols
    place_high = (level * 2 + owner_row % 2).astype(F32)
    place_low = within.astype(F32)
    pair_iota = lax.broadcasted_iota(jnp.int32, (pairs, local_rows), 0)
    member = pair_iota == pair
    member_f = jnp.where(member, 1.0, 0.0)
    counts = jnp.dot(member_f.astype(BF16), before, preferred_element_type=F32)
    rank = jnp.sum(member_f * counts, axis=0, keepdims=True).astype(jnp.int32)
    slot = pair * chunk_rows + rank
    chosen = lax.broadcasted_iota(jnp.int32, (local_rows, local_rows), 0) == slot
    tail = total_rows - chunk_rows
    tail_iota = lax.broadcasted_iota(jnp.int32, (pairs * tail, local_rows), 0)
    tail_pair = tail_iota // tail
    tail_row = tail_iota % tail
    tail_value = jnp.where(tail_row == 0, place_high, jnp.where(tail_row == 1, place_low, 0.0))
    tail_value = jnp.where(tail_pair == pair, tail_value, 0.0).astype(BF16)
    lane = rank + (me % shards_per_line) * chunk_rows
    lane_hot = lax.broadcasted_iota(jnp.int32, (LANES, local_rows), 0) == lane
    tails = lax.dot_general(
        tail_value,
        jnp.where(lane_hot, 1.0, 0.0).astype(BF16),
        (((1,), (1,)), ((), ())),
        preferred_element_type=F32,
    )
    rhs_copy.wait()
    sorted_rows = jnp.dot(
        jnp.where(chosen, 1.0, 0.0).astype(BF16),
        rhs_ref[...].astype(BF16),
        preferred_element_type=F32,
    )
    half = rhs_ref.shape[1] // 2
    for g in range(pairs):
        chosen_rows = sorted_rows[g * chunk_rows : (g + 1) * chunk_rows]
        ending = tails[g * tail : (g + 1) * tail]
        for h in range(2):
            side = chosen_rows[:, h * half : (h + 1) * half]
            chunk = jnp.concatenate([side, ending], axis=0)
            out_ref[(2 * (g // cols) + h) * cols + g % cols] = chunk.astype(BF16)


def place_rows(arrived_ref, first_place, place_count, chunk_rows):
    shards = arrived_ref.shape[0]
    shards_per_line = LANES // chunk_rows
    hots = []
    place = lax.broadcasted_iota(jnp.int32, (place_count, LANES), 0) + first_place
    for first in range(0, shards, shards_per_line):
        ending = jnp.zeros((8, LANES), F32)
        for s in range(first, first + shards_per_line):
            ending = ending + arrived_ref[s].astype(F32)[chunk_rows : chunk_rows + 8]
        where_to = (ending[0:1] * B + ending[1:2]).astype(jnp.int32)
        hots.append(jnp.where(place == where_to, 1.0, 0.0).astype(BF16))
    hot = jnp.concatenate(hots, axis=1)
    rows = jnp.concatenate(
        [arrived_ref[s].astype(F32)[:chunk_rows] for s in range(shards)], axis=0
    ).astype(BF16)
    return lax.dot_general(
        rows, hot, (((0,), (1,)), ((), ())), preferred_element_type=F32
    ).astype(BF16)


def times(left, right):
    return jnp.dot(left, right, preferred_element_type=F32)


def times_t(left, right):
    return lax.dot_general(left, right, (((1,), (1,)), ((), ())), preferred_element_type=F32)


def apply_diag(product, level, residual, own_ref, par_ref, out_ref):
    parity = lax.axis_index("row") % 2
    for at, factor in ((parity, own_ref), (1 - parity, par_ref)):
        lanes = aligned(at, B, B)
        out_ref[:, lanes] = product(residual[:, lanes], factor[level]).astype(BF16)


def first_body(chunk_rows, arrived_ref, own_ref, par_ref, out_ref, residual):
    residual[...] = place_rows(arrived_ref, 0, 2 * B, chunk_rows)
    apply_diag(times_t, 0, residual, own_ref, par_ref, out_ref)


def rest_body(chunk_rows, arrived_ref, *outs):
    placed = place_rows(arrived_ref, 2 * B, len(outs) * 2 * B, chunk_rows)
    for k, out in enumerate(outs):
        out[...] = placed[:, k * 2 * B : (k + 1) * 2 * B]


def gather_pieces(pieces, position, gathered):
    for m, piece in enumerate(pieces):
        gathered[:, aligned(position ^ m, 2 * B, 2 * B)] = piece[...]


def down_body(tile_ref, *refs, groups, distances):
    pieces, outs, gathered = refs[:groups], refs[groups:-1], refs[-1]
    col = lax.axis_index("col")
    gather_pieces(pieces, lax.axis_index("row") // 2, gathered)
    for m, out in zip(distances, outs):
        at = aligned(col ^ m, 2 * B, 2 * B)
        out[...] = times(gathered[...], tile_ref[:, at]).astype(out.dtype)


def up_body(tile_ref, *refs, cols, distances):
    pieces, outs, gathered = refs[:cols], refs[cols:-1], refs[-1]
    group = lax.axis_index("row") // 2
    gather_pieces(pieces, lax.axis_index("col"), gathered)
    for m, out in zip(distances, outs):
        at = aligned(group ^ m, 2 * B, 2 * B)
        out[...] = times(gathered[...], tile_ref[:, at]).astype(out.dtype)


def split_off(block_ref, theirs_ref):
    theirs_ref[...] = block_ref[:, aligned(1 - lax.axis_index("row") % 2, B, B)]


def finish_body(*refs):
    blocks, others, out_ref = refs[:NLEV], refs[NLEV], refs[-1]
    parity = lax.axis_index("row") % 2
    mine, other = aligned(parity, B, B), aligned(1 - parity, B, B)
    for level in range(NLEV):
        out_ref[level, 0, :, mine] = blocks[level][:, mine].T
        if level:
            out_ref[level, 0, :, other] = others[:, (level - 1) * B : level * B].T


def last_body(started_ref, other_ref, out_ref, turned, sem):
    turned[...] = other_ref[...].T
    lanes = aligned(1 - lax.axis_index("row") % 2, B, B)
    copy = pltpu.make_async_copy(turned, out_ref.at[0, 0, :, lanes], sem)
    copy.start()
    copy.wait()


def residual_body(rhs_ref, own_ref, par_ref, kept_ref, *refs, level):
    last = level == NLEV - 1
    if last:
        arrived, outs, theirs, residual, solved = refs[:-4], *refs[-4:]
    else:
        arrived, solved, residual = refs[:-2], refs[-2], refs[-1]
    coupled = kept_ref[...]
    for ref in arrived:
        coupled = coupled + ref[...].astype(F32)
    residual[...] = (rhs_ref[...].astype(F32) - coupled).astype(BF16)
    apply_diag(times_t, level, residual, own_ref, par_ref, solved)
    if last:
        apply_diag(times, level, solved, own_ref, par_ref, outs)
        split_off(outs, theirs)


def final_body(solved_ref, own_ref, par_ref, kept_ref, *refs, level):
    arrived, outs, theirs, residual = refs[:-3], *refs[-3:]
    back = kept_ref[...]
    for ref in arrived:
        back = back + ref[...].astype(F32)
    residual[...] = (solved_ref[...].astype(F32) - back).astype(BF16)
    apply_diag(times, level, residual, own_ref, par_ref, outs)
    split_off(outs, theirs)


def per_device(rhs_rows, dest_row, diag_inverse, lower_blocks, block_mask):
    rows = lax.axis_size("row")
    cols = lax.axis_size("col")
    groups = rows // 2
    supernodes = rows * cols
    local_rows = rhs_rows.shape[0]
    half = rhs_rows.shape[1] // 2
    chunk_rows = 2 * (local_rows // supernodes)
    total_rows = (chunk_rows + 2 + 7) // 8 * 8

    def shape(dims, dtype=BF16):
        return jax.ShapeDtypeStruct(dims, dtype)

    diag_own = diag_inverse[:, 0]
    diag_par = swap(diag_own, "row", 1)
    own, par = [], [None] * (NLEV - 1)
    for level in range(NLEV - 1):
        tile = lower_blocks[level, 0, :, :, 0]
        mask = block_mask[level, 0, :, 0, :].astype(BF16)
        masked = (tile * mask[:, None, :, None]).reshape(cols * B, rows * B)
        own.append(masked)

    sending = call(
        functools.partial(pack_body, rows, cols, chunk_rows, total_rows),
        shape((supernodes, total_rows, half)),
        (rhs_rows, dest_row.reshape(1, local_rows)),
        [
            pltpu.VMEM(rhs_rows.shape, F32),
            pltpu.VMEM((1, local_rows), jnp.int32),
            pltpu.SemaphoreType.DMA((2,)),
        ],
        space=pl.ANY,
        limit=60 * 1024 * 1024,
        flops=2 * local_rows * local_rows * 2 * half,
    )
    arrived = lax.all_to_all(sending, ("row", "col"), split_axis=0, concat_axis=0, tiled=True)
    block = (half, 2 * B)
    solved = [
        call(
            functools.partial(first_body, chunk_rows),
            shape(block),
            (arrived, diag_own, diag_par),
            [pltpu.VMEM(block, BF16)],
        )
    ]
    rest = call(
        functools.partial(rest_body, chunk_rows),
        [shape(block) for _ in range(NLEV - 1)],
        (arrived,),
    )
    upper = None
    for level in range(1, NLEV):
        if level == 1:
            own[0], _ = lax.optimization_barrier((own[0], solved[0]))
            par[0] = swap(own[0], "row", 1)
        if level < NLEV - 1:
            own[level], _ = lax.optimization_barrier((own[level], solved[-1]))
            par[level] = swap(own[level], "row", 1)
        sent = {
            m: swap(solved[-1], "row", 2 * m) for m in reversed(issue_order(groups, ROW_ORDER))
        }
        pieces = [solved[-1]] + [sent[m] for m in range(1, groups)]
        tiles = fetch_turned(own[level - 1], par[level - 1], solved[-1])
        far = list(range(1, cols))
        sums = [
            call(
                functools.partial(down_body, groups=groups, distances=distances),
                [shape(block, F32 if m == 0 else BF16) for m in distances],
                (tiles, *pieces),
                [pltpu.VMEM((half, rows * B), BF16)],
                flops=4 * rows * B * B * half * len(distances),
            )
            for distances in (far, [0])
        ]
        sums = [*sums[1], *sums[0]]
        passed = [swap(sums[m], "col", m) for m in issue_order(cols, COL_ORDER)]
        last = level == NLEV - 1
        result = call(
            functools.partial(residual_body, level=level),
            [shape(block), shape((half, B))] if last else shape(block),
            (rest[level - 1], diag_own, diag_par, sums[0], *passed),
            [pltpu.VMEM(block, BF16)] * (2 if last else 1),
        )
        if last:
            upper, theirs = result
        else:
            solved.append(result)

    solution, leaving = [None] * NLEV, [None] * NLEV
    solution[NLEV - 1], leaving[NLEV - 1] = upper, theirs
    for level in range(NLEV - 2, -1, -1):
        sent = {m: swap(upper, "col", m) for m in reversed(issue_order(cols, TURN_ORDER))}
        pieces = [upper] + [sent[m] for m in range(1, cols)]
        tiles = fetch(own[level], par[level], upper)
        far = list(range(1, groups))
        sums = [
            call(
                functools.partial(up_body, cols=cols, distances=distances),
                [shape(block, F32 if m == 0 else BF16) for m in distances],
                (tiles, *pieces),
                [pltpu.VMEM((half, 2 * cols * B), BF16)],
                flops=4 * cols * B * B * half * len(distances),
            )
            for distances in (far, [0])
        ]
        sums = [*sums[1], *sums[0]]
        passed = [swap(sums[m], "row", 2 * m) for m in issue_order(groups, ROW_ORDER)]
        upper, theirs = call(
            functools.partial(final_body, level=level),
            [shape(block), shape((half, B))],
            (solved[level], diag_own, diag_par, sums[0], *passed),
            [pltpu.VMEM(block, BF16)],
        )
        solution[level], leaving[level] = upper, theirs

    others = swap(jnp.concatenate(leaving[1:], axis=1), "row", 1)
    first_other = swap(leaving[0], "row", 1)
    started = call(finish_body, shape((NLEV, 1, B, 2 * half)), (*solution, others))
    return pl.pallas_call(
        last_body,
        out_shape=shape((NLEV, 1, B, 2 * half)),
        in_specs=[pl.BlockSpec(memory_space=pl.ANY), pl.BlockSpec(memory_space=pltpu.VMEM)],
        out_specs=pl.BlockSpec(memory_space=pl.ANY),
        scratch_shapes=[pltpu.VMEM((B, half), BF16), pltpu.SemaphoreType.DMA],
        input_output_aliases={0: 0},
        compiler_params=pltpu.CompilerParams(vmem_limit_bytes=VMEM_BYTES),
    )(started, first_other)


def solution(mesh):
    in_specs = (
        P(("row", "col"), None),
        P(("row", "col")),
        P(None, ("row", "col"), None, None),
        P(None, "row", None, None, "col", None, None),
        P(None, "row", None, "col", None),
    )
    out_specs = P(None, ("row", "col"), None, None)
    return jax.shard_map(
        per_device, mesh=mesh, in_specs=in_specs, out_specs=out_specs, check_vma=False
    )
```
